128 devices in a mesh: ty: 16 (over z, y_lo, core), tx: 8 (over x, y_hi).
Axes of the slice: x: 4, y: 4 (y_hi: 2, y_lo: 2; y = y_hi * 2 + y_lo), z: 4, core: 2. Of those that a mesh axis runs over, the one named last changes fastest.
Arguments:
- object_field: float32 [2, 8192, 4096], P(None, 'ty', 'tx'), may hold values from -6 to 6
- probe: float32 [2, 256, 256], replicated, may hold values from -3 to 3
- measured: float32 [2048, 256, 256], P(('ty', 'tx')), may hold values from 0.1 to 4
- offsets: int32 [2048, 2], P(('ty', 'tx')), may hold values from 0 to 511, as said below
- live: int32 [128], P(('ty', 'tx')), may hold values from 1 to 16, as said below
Outputs:
- object_new: float32 [2, 8192, 4096], P(None, 'ty', 'tx')
- probe_new: float32 [2, 256, 256], replicated
The draws below stay inside these ranges and needn't reach their ends.
Inputs may be any that keep to these rules, and one draw needn't show every extreme that they name: `offsets`: every patch lies inside the object. `live`: used slots come first in each owner's slots; some owner uses all 16.
All inputs are finite; a program needn't handle non-finite values.
Results may differ from the reference program's by a relative error of at most 0.0003.
Values sent between devices are 32-bit elements; how exact they have to be, the bound alone decides.
No kernel may reach another device: no remote copies, remote signals or barrier semaphores. Data moves between devices by JAX's collectives and lax.ppermute only.
A program may use at most 128 MiB of HBM per device.

```python
import math
import jax
import jax.numpy as jnp
from jax import lax

P_SIZE = 256
TILE = 512
SLOTS = 16
NR = 8192
NC = 4096
POSITIONS = 2048
N_TY = 16
N_TX = 8


def draw_offsets(key, part):
    key = jax.random.fold_in(key, 11)
    first, second = jax.random.split(key)
    numbers = jnp.arange(POSITIONS, dtype=jnp.int32)
    blocks = numbers // SLOTS
    tile_rows = blocks // N_TX
    tile_cols = blocks % N_TX
    limit_rows = jnp.where(tile_rows == N_TY - 1, TILE - P_SIZE, TILE - 1) + 1
    limit_cols = jnp.where(tile_cols == N_TX - 1, TILE - P_SIZE, TILE - 1) + 1
    rows = jax.random.randint(first, (POSITIONS,), 0, limit_rows, dtype=jnp.int32)
    cols = jax.random.randint(second, (POSITIONS,), 0, limit_cols, dtype=jnp.int32)
    rows = rows.at[0].set(TILE - 1).at[1].set(0)
    cols = cols.at[0].set(TILE - 1).at[1].set(0)
    return jnp.stack([rows, cols], axis=1)


def draw_live(key, part):
    key = jax.random.fold_in(key, 12)
    first, second = jax.random.split(key)
    owners = N_TY * N_TX
    counts = jax.random.randint(first, (owners,), 1, SLOTS + 1, dtype=jnp.int32)
    chosen = jax.random.randint(second, (), 0, owners, dtype=jnp.int32)
    lowest = (chosen + 1) % owners
    return counts.at[chosen].set(SLOTS).at[lowest].set(1)


def steps_of(key, dims, pieces, least, top_value):
    gain, own = 1.0, jax.random.fold_in(key, 6)
    for axis_at, blocks in pieces:
        steps = jnp.exp(jax.random.uniform(jax.random.fold_in(own, axis_at), (blocks,), jnp.float32, least / len(pieces), top_value / len(pieces)))
        gain = gain * jnp.repeat(steps, dims[axis_at] // blocks).reshape([-1 if axis == axis_at else 1 for axis in range(len(dims))])
    return gain


def centred(rng, extent, width, reach, pieces=(), kind=jnp.bfloat16):
    gain = steps_of(rng, extent, pieces, -0.22, 0.18) if pieces else 1.0
    values = jax.random.normal(rng, extent, jnp.float32) * width * gain
    return jnp.minimum(jnp.maximum(values, -reach), reach).astype(kind)


def setup_inputs(seed: int = 0) -> dict:
    key_list = jax.random.split(jax.random.key(seed), 6)
    object_field = centred(key_list[0], (2, NR, NC), 1.0, 6.0, ((1, 16), (2, 8)), jnp.float32)
    probe = centred(key_list[1], (2, P_SIZE, P_SIZE), 0.5, 3.0, (), jnp.float32)
    measured = jnp.clip(jnp.exp(math.log(4.0) - 3.6888794 * jax.random.uniform(key_list[2], (POSITIONS, P_SIZE, P_SIZE), jnp.float32) ** steps_of(key_list[2], (POSITIONS, P_SIZE, P_SIZE), ((0, 128),), -0.2, 0.2)), 0.1, 4.0)
    offsets = draw_offsets(jax.random.fold_in(key_list[5], 71), 0)
    live = draw_live(jax.random.fold_in(key_list[5], 71), 0)
    return dict(object_field=object_field, probe=probe, measured=measured, offsets=offsets, live=live)


def reference(object_field, probe, measured, offsets, live):
    complex_object = lax.complex(object_field[0], object_field[1])
    complex_probe = lax.complex(probe[0], probe[1])

    def visit(carry, inputs):
        grad_object, grad_probe = carry
        number, offset, pattern = inputs
        block = number // SLOTS
        slot = number % SLOTS
        row = (block // N_TX * TILE + offset[0]).astype(jnp.int32)
        col = (block % N_TX * TILE + offset[1]).astype(jnp.int32)
        weight = (slot < live[block]).astype(object_field.dtype)
        patch = lax.dynamic_slice(complex_object, (row, col), (P_SIZE, P_SIZE))
        far = jnp.fft.fft2(complex_probe * patch, norm='ortho')
        misfit = (far.real * far.real + far.imag * far.imag - pattern) * weight
        back = jnp.fft.ifft2(misfit * far, norm='ortho')
        current = lax.dynamic_slice(grad_object, (row, col), (P_SIZE, P_SIZE))
        grad_object = lax.dynamic_update_slice(grad_object, current + jnp.conj(complex_probe) * back, (row, col))
        return ((grad_object, grad_probe + jnp.conj(patch) * back), None)
    numbers = jnp.arange(POSITIONS, dtype=jnp.int32)
    start = (jnp.zeros_like(complex_object), jnp.zeros_like(complex_probe))
    (grad_object, grad_probe), unused = lax.scan(visit, start, (numbers, offsets, measured))
    object_next = complex_object - 0.25 * grad_object
    probe_next = complex_probe - 1.0 / math.sqrt(POSITIONS) * grad_probe
    return (jnp.stack([object_next.real, object_next.imag]), jnp.stack([probe_next.real, probe_next.imag]))
```

```python
import functools
import math

import jax
import jax.numpy as jnp
import ml_dtypes
import numpy as np
from jax import lax
from jax.experimental import pallas as pl
from jax.experimental.pallas import tpu as pltpu
from jax.sharding import PartitionSpec as P

BF16 = jnp.bfloat16
F32 = jnp.float32
SIDE = 256
HALF = 128
TILE = 512
WIDE = TILE + SIDE
ROWS = 64


def split_np(table):
    high = table.astype(ml_dtypes.bfloat16)
    low = (table - high.astype(np.float64)).astype(ml_dtypes.bfloat16)
    return high, low


def dft_tables():
    k = np.arange(HALF)[:, None]
    n = np.arange(HALF)[None, :]
    forward = []
    backward = []
    for parity in range(2):
        angle = -2.0 * math.pi * ((n * (2 * k + parity)) % SIDE) / SIDE
        cos = np.cos(angle) / math.sqrt(SIDE)
        sin = np.sin(angle) / math.sqrt(SIDE)
        stacked = np.block([[cos, -sin], [sin, cos]])
        forward.extend(split_np(stacked))
        backward.extend(split_np(stacked.T))
    tables = np.stack(forward + backward).reshape(2, 2, 2, SIDE, SIDE)
    order = np.concatenate([np.arange(0, SIDE, 2), np.arange(1, SIDE, 2)])
    select = np.zeros((SIDE, SIDE), np.float32)
    select[order, np.arange(SIDE)] = 1.0
    return tables, select.astype(ml_dtypes.bfloat16)


def split(x):
    high = x.astype(BF16)
    low = (x - high.astype(F32)).astype(BF16)
    return high, low


def mm(a, b):
    return lax.dot_general(a, b, (((1,), (0,)), ((), ())), preferred_element_type=F32)


def left3(high, low, x_high, x_low):
    return mm(high, x_high) + (mm(high, x_low) + mm(low, x_high))


def right3(x_high, x_low, high, low):
    return mm(x_high, high) + (mm(x_low, high) + mm(x_high, low))


def one_slot(r, c, ext, grad, probe, pgrad, tab, sel, meas, patch, xh, xl, fa, fb):
    j = c // HALF
    s = c % HALF
    back_shift = lax.rem(HALF - s, HALF)
    lane = lax.broadcasted_iota(jnp.int32, (ROWS, HALF), 1)
    take_first = lane < HALF - s
    below_shift = lane < s

    for rc in range(0, HALF, ROWS):
        wave = []
        for t in range(2):
            cut = []
            for part in range(2):
                rolled = [
                    pltpu.roll(ext[part, j + h, pl.ds(r + t * HALF + rc, ROWS), :], back_shift, 1) for h in range(3)
                ]
                halves = [jnp.where(take_first, rolled[h], rolled[h + 1]) for h in range(2)]
                for h in range(2):
                    patch[part, h, pl.ds(t * HALF + rc, ROWS), :] = halves[h]
                cut.append(halves)
            rows = pl.ds(t * HALF + rc, ROWS)
            here = []
            for h in range(2):
                cols = pl.ds(h * HALF, HALF)
                qr = probe[0, rows, cols]
                qi = probe[1, rows, cols]
                here.append((qr * cut[0][h] - qi * cut[1][h], qr * cut[1][h] + qi * cut[0][h]))
            wave.append(here)
        for h in range(2):
            for part in range(2):
                top = wave[0][h][part]
                bottom = wave[1][h][part]
                for p, folded in enumerate((top + bottom, top - bottom)):
                    high, low = split(folded)
                    xh[p, pl.ds(part * HALF + rc, ROWS), pl.ds(h * HALF, HALF)] = high
                    xl[p, pl.ds(part * HALF + rc, ROWS), pl.ds(h * HALF, HALF)] = low

    for p in range(2):
        fa[p] = left3(tab[0, p, 0], tab[0, p, 1], xh[p], xl[p])

    for p in range(2):
        for h in range(2):
            high, low = split(meas[h, pl.ds(p, HALF, stride=2), :])
            xh[2, pl.ds(p * HALF, HALF), pl.ds(h * HALF, HALF)] = high
            xl[2, pl.ds(p * HALF, HALF), pl.ds(h * HALF, HALF)] = low
    fb[2] = mm(xh[2], sel[...]) + mm(xl[2], sel[...])

    for p in range(2):
        for rc in range(0, HALF, ROWS):
            for part in range(2):
                rows = pl.ds(part * HALF + rc, ROWS)
                near = fa[p, rows, pl.ds(0, HALF)]
                far = fa[p, rows, pl.ds(HALF, HALF)]
                for q, folded in enumerate((near + far, near - far)):
                    high, low = split(folded)
                    xh[3 + q, pl.ds(p * HALF + rc, ROWS), pl.ds(part * HALF, HALF)] = high
                    xl[3 + q, pl.ds(p * HALF + rc, ROWS), pl.ds(part * HALF, HALF)] = low

    for q in range(2):
        fb[q] = right3(xh[3 + q], xl[3 + q], tab[1, q, 0], tab[1, q, 1])

    for q in range(2):
        for rc in range(0, SIDE, ROWS):
            rows = pl.ds(rc, ROWS)
            re = fb[q, rows, pl.ds(0, HALF)]
            im = fb[q, rows, pl.ds(HALF, HALF)]
            misfit = re * re + im * im - fb[2, rows, pl.ds(q * HALF, HALF)]
            for part, value in enumerate((misfit * re, misfit * im)):
                high, low = split(value)
                xh[5 + q, rows, pl.ds(part * HALF, HALF)] = high
                xl[5 + q, rows, pl.ds(part * HALF, HALF)] = low

    for q in range(2):
        fa[2 + q] = right3(xh[5 + q], xl[5 + q], tab[0, q, 0], tab[0, q, 1])

    for p in range(2):
        for rc in range(0, HALF, ROWS):
            rows = pl.ds(p * HALF + rc, ROWS)
            for part in range(2):
                cols = pl.ds(part * HALF, HALF)
                even = fa[2, rows, cols]
                odd = fa[3, rows, cols]
                for h, value in enumerate((even + odd, even - odd)):
                    high, low = split(value)
                    xh[7 + p, pl.ds(part * HALF + rc, ROWS), pl.ds(h * HALF, HALF)] = high
                    xl[7 + p, pl.ds(part * HALF + rc, ROWS), pl.ds(h * HALF, HALF)] = low

    for p in range(2):
        fb[3 + p] = left3(tab[1, p, 0], tab[1, p, 1], xh[7 + p], xl[7 + p])

    for rc in range(0, HALF, ROWS):
        for t in range(2):
            rows = pl.ds(t * HALF + rc, ROWS)
            pieces = []
            for h in range(2):
                cols = pl.ds(h * HALF, HALF)
                er = fb[3, pl.ds(rc, ROWS), cols]
                ei = fb[3, pl.ds(HALF + rc, ROWS), cols]
                dr = fb[4, pl.ds(rc, ROWS), cols]
                di = fb[4, pl.ds(HALF + rc, ROWS), cols]
                br, bi = (er + dr, ei + di) if t == 0 else (er - dr, ei - di)
                qr = probe[0, rows, cols]
                qi = probe[1, rows, cols]
                pr = patch[0, h, rows, :]
                pi = patch[1, h, rows, :]
                pgrad[0, rows, cols] += pr * br + pi * bi
                pgrad[1, rows, cols] += pr * bi - pi * br
                pieces.append((qr * br + qi * bi, qr * bi - qi * br))
            target = pl.ds(r + t * HALF + rc, ROWS)
            for part in range(2):
                first = pltpu.roll(pieces[0][part], s, 1)
                second = pltpu.roll(pieces[1][part], s, 1)
                grad[part, j, target, :] += jnp.where(below_shift, 0.0, first)
                grad[part, j + 1, target, :] += jnp.where(below_shift, first, second)
                grad[part, j + 2, target, :] += jnp.where(below_shift, second, 0.0)


def kernel(
    count, offsets, own, right, below, corner, probe, measured, tab, sel,
    own_out, right_out, below_out, corner_out, pgrad,
    ext, grad, meas, patch, xh, xl, fa, fb, sems, msems, osems,
):
    parts = []
    for part in range(2):
        for h in range(4):
            parts.append((own.at[part, :, pl.ds(h * HALF, HALF)], ext.at[part, h, pl.ds(0, TILE), :]))
            parts.append((below.at[part, :, pl.ds(h * HALF, HALF)], ext.at[part, h, pl.ds(TILE, SIDE), :]))
        for h in range(2):
            parts.append((right.at[part, :, pl.ds(h * HALF, HALF)], ext.at[part, 4 + h, pl.ds(0, TILE), :]))
            parts.append((corner.at[part, :, pl.ds(h * HALF, HALF)], ext.at[part, 4 + h, pl.ds(TILE, SIDE), :]))
    loads = [pltpu.make_async_copy(a, b, sems.at[i]) for i, (a, b) in enumerate(parts)]
    for load in loads:
        load.start()

    def fetch(g, slot):
        return [
            pltpu.make_async_copy(measured.at[g, :, pl.ds(h * HALF, HALF)], meas.at[slot, h], msems.at[slot, h])
            for h in range(2)
        ]

    for copy in fetch(0, 0):
        copy.start()
    grad[...] = jnp.zeros_like(grad)
    pgrad[...] = jnp.zeros_like(pgrad)
    for load in loads:
        load.wait()
    total = count[0]

    def step(g, carry):
        slot = lax.rem(g, 2)

        @pl.when(g + 1 < total)
        def _():
            for copy in fetch(g + 1, 1 - slot):
                copy.start()

        for copy in fetch(g, slot):
            copy.wait()
        one_slot(
            offsets[2 * g], offsets[2 * g + 1], ext, grad, probe, pgrad, tab, sel, meas.at[slot],
            patch, xh, xl, fa, fb,
        )
        return carry

    lax.fori_loop(0, total, step, 0)

    parts = []
    for part in range(2):
        for h in range(4):
            parts.append((grad.at[part, h, pl.ds(0, TILE), :], own_out.at[part, :, pl.ds(h * HALF, HALF)]))
            parts.append((grad.at[part, h, pl.ds(TILE, SIDE), :], below_out.at[part, :, pl.ds(h * HALF, HALF)]))
        for h in range(2):
            parts.append((grad.at[part, 4 + h, pl.ds(0, TILE), :], right_out.at[part, :, pl.ds(h * HALF, HALF)]))
            parts.append((grad.at[part, 4 + h, pl.ds(TILE, SIDE), :], corner_out.at[part, :, pl.ds(h * HALF, HALF)]))
    stores = [pltpu.make_async_copy(a, b, osems.at[i]) for i, (a, b) in enumerate(parts)]
    for store in stores:
        store.start()
    for store in stores:
        store.wait()


def slots_call(count, offsets, own, right, below, corner, probe, measured):
    tables, select = dft_tables()
    any_spec = pl.BlockSpec(memory_space=pl.ANY)
    smem = pl.BlockSpec(memory_space=pltpu.SMEM)
    vmem = pl.BlockSpec(memory_space=pltpu.VMEM)
    shapes = [own.shape, right.shape, below.shape, corner.shape, probe.shape]
    return pl.pallas_call(
        kernel,
        out_shape=[jax.ShapeDtypeStruct(s, F32) for s in shapes],
        in_specs=[smem, smem, any_spec, any_spec, any_spec, any_spec, vmem, any_spec, vmem, vmem],
        out_specs=[any_spec] * 4 + [vmem],
        scratch_shapes=[
            pltpu.VMEM((2, 6, WIDE, HALF), F32),
            pltpu.VMEM((2, 6, WIDE, HALF), F32),
            pltpu.VMEM((2, 2, SIDE, HALF), F32),
            pltpu.VMEM((2, 2, SIDE, HALF), F32),
            pltpu.VMEM((9, SIDE, SIDE), BF16),
            pltpu.VMEM((9, SIDE, SIDE), BF16),
            pltpu.VMEM((4, SIDE, SIDE), F32),
            pltpu.VMEM((5, SIDE, SIDE), F32),
            pltpu.SemaphoreType.DMA((24,)),
            pltpu.SemaphoreType.DMA((2, 2)),
            pltpu.SemaphoreType.DMA((24,)),
        ],
        compiler_params=pltpu.CompilerParams(vmem_limit_bytes=40 * 1024 * 1024),
        cost_estimate=pl.CostEstimate(flops=16 * 26 * 2 * SIDE**3, bytes_accessed=20 * 2**20, transcendentals=0),
    )(count, offsets.reshape(-1), own, right, below, corner, probe, measured, jnp.asarray(tables), jnp.asarray(select))


def passed_along(block, axis, distance):
    devices = range(lax.axis_size(axis))
    route = [(i - distance, i) for i in devices if i - distance in devices]
    return lax.ppermute(block, axis, route)


def total_over_all(x):
    axes = ("ty", "tx")
    devices = lax.axis_size("ty") * lax.axis_size("tx")
    shares = lax.all_to_all(x.reshape(devices, -1), axes, 0, 0, tiled=True)
    share = jnp.sum(shares, axis=0, keepdims=True)
    copies = jnp.broadcast_to(share, shares.shape)
    return lax.all_to_all(copies, axes, 0, 0, tiled=True).reshape(x.shape)


def body(object_field, probe, measured, offsets, live):
    side = probe.shape[1]
    tile = object_field.shape[1]
    right = passed_along(object_field[:, :, :side], "tx", -1)
    below = passed_along(object_field[:, :side, :], "ty", -1)
    corner = passed_along(right[:, :side, :], "ty", -1)
    own_grad, right_grad, below_grad, corner_grad, probe_grad = slots_call(
        live, offsets, object_field, right, below, corner, probe, measured
    )
    from_corner = passed_along(corner_grad, "ty", 1)
    from_above = passed_along(below_grad, "ty", 1)
    from_left = passed_along(right_grad.at[:, :side, :].add(from_corner), "tx", 1)
    total_grad = total_over_all(probe_grad)
    own_grad = own_grad.at[:, :side, :].add(from_above).at[:, :, :side].add(from_left)
    object_next = object_field - 0.25 * own_grad
    positions = measured.shape[0] * lax.axis_size("ty") * lax.axis_size("tx")
    probe_next = probe - (1.0 / math.sqrt(positions)) * total_grad
    return (object_next, probe_next)


def solution(mesh):
    placed = (
        P(None, "ty", "tx"),
        P(),
        P(("ty", "tx"), None, None),
        P(("ty", "tx"), None),
        P(("ty", "tx")),
    )
    return jax.shard_map(
        body, mesh=mesh, in_specs=placed, out_specs=(P(None, "ty", "tx"), P()), check_vma=False
    )
```

```python
import functools
import math

import jax
import jax.numpy as jnp
import ml_dtypes
import numpy as np
from jax import lax
from jax.experimental import pallas as pl
from jax.experimental.pallas import tpu as pltpu
from jax.sharding import PartitionSpec as P

BF16 = jnp.bfloat16
F32 = jnp.float32
SIDE = 256
HALF = 128
TILE = 512
WIDE = TILE + SIDE
ROWS = 64


def split_np(table):
    high = table.astype(ml_dtypes.bfloat16)
    low = (table - high.astype(np.float64)).astype(ml_dtypes.bfloat16)
    return high, low


def dft_tables():
    k = np.arange(HALF)[:, None]
    n = np.arange(HALF)[None, :]
    forward = []
    backward = []
    for parity in range(2):
        angle = -2.0 * math.pi * ((n * (2 * k + parity)) % SIDE) / SIDE
        cos = np.cos(angle) / math.sqrt(SIDE)
        sin = np.sin(angle) / math.sqrt(SIDE)
        stacked = np.block([[cos, -sin], [sin, cos]])
        forward.extend(split_np(stacked))
        backward.extend(split_np(stacked.T))
    tables = np.stack(forward + backward).reshape(2, 2, 2, SIDE, SIDE)
    order = np.concatenate([np.arange(0, SIDE, 2), np.arange(1, SIDE, 2)])
    select = np.zeros((SIDE, SIDE), np.float32)
    select[order, np.arange(SIDE)] = 1.0
    return tables, select.astype(ml_dtypes.bfloat16)


def split(x):
    high = x.astype(BF16)
    low = (x - high.astype(F32)).astype(BF16)
    return high, low


def mm(a, b):
    return lax.dot_general(a, b, (((1,), (0,)), ((), ())), preferred_element_type=F32)


def left3(high, low, x_high, x_low):
    return mm(high, x_high) + (mm(high, x_low) + mm(low, x_high))


def right3(x_high, x_low, high, low):
    return mm(x_high, high) + (mm(x_low, high) + mm(x_high, low))


def cut_steps(r, c, ext, probe, patch, xh, xl):
    j = c // HALF
    back_shift = lax.rem(HALF - c % HALF, HALF)
    lane = lax.broadcasted_iota(jnp.int32, (ROWS, HALF), 1)
    take_first = lane < HALF - c % HALF

    def chunk(rc):
        wave = []
        for t in range(2):
            cut = []
            rows = pl.ds(t * HALF + rc, ROWS)
            for part in range(2):
                rolled = [
                    pltpu.roll(ext[part, j + h, pl.ds(r + t * HALF + rc, ROWS), :], back_shift, 1) for h in range(3)
                ]
                halves = [jnp.where(take_first, rolled[h], rolled[h + 1]) for h in range(2)]
                for h in range(2):
                    patch[part, h, rows, :] = halves[h]
                cut.append(halves)
            here = []
            for h in range(2):
                cols = pl.ds(h * HALF, HALF)
                qr = probe[0, rows, cols]
                qi = probe[1, rows, cols]
                here.append((qr * cut[0][h] - qi * cut[1][h], qr * cut[1][h] + qi * cut[0][h]))
            wave.append(here)
        for h in range(2):
            for part in range(2):
                top = wave[0][h][part]
                bottom = wave[1][h][part]
                for p, folded in enumerate((top + bottom, top - bottom)):
                    high, low = split(folded)
                    xh[p, pl.ds(part * HALF + rc, ROWS), pl.ds(h * HALF, HALF)] = high
                    xl[p, pl.ds(part * HALF + rc, ROWS), pl.ds(h * HALF, HALF)] = low

    return [functools.partial(chunk, rc) for rc in range(0, HALF, ROWS)]


def transform_steps(meas, tab, sel, xh, xl, fa, fb):
    first, middle = [], []

    def left(out, k, table, p, source):
        out[k] = left3(tab[table, p, 0], tab[table, p, 1], xh[source], xl[source])

    def right(out, k, table, q, source):
        out[k] = right3(xh[source], xl[source], tab[table, q, 0], tab[table, q, 1])

    def sort_measured(p, h):
        high, low = split(meas[h, pl.ds(p, HALF, stride=2), :])
        xh[2, pl.ds(p * HALF, HALF), pl.ds(h * HALF, HALF)] = high
        xl[2, pl.ds(p * HALF, HALF), pl.ds(h * HALF, HALF)] = low

    def select():
        fb[2] = mm(xh[2], sel[...]) + mm(xl[2], sel[...])

    def fold_cols(p, rc):
        for part in range(2):
            rows = pl.ds(part * HALF + rc, ROWS)
            near = fa[p, rows, pl.ds(0, HALF)]
            far = fa[p, rows, pl.ds(HALF, HALF)]
            for q, folded in enumerate((near + far, near - far)):
                high, low = split(folded)
                xh[3 + q, pl.ds(p * HALF + rc, ROWS), pl.ds(part * HALF, HALF)] = high
                xl[3 + q, pl.ds(p * HALF + rc, ROWS), pl.ds(part * HALF, HALF)] = low

    def misfit(q, rc):
        rows = pl.ds(rc, ROWS)
        re = fb[q, rows, pl.ds(0, HALF)]
        im = fb[q, rows, pl.ds(HALF, HALF)]
        miss = re * re + im * im - fb[2, rows, pl.ds(q * HALF, HALF)]
        for part, value in enumerate((miss * re, miss * im)):
            high, low = split(value)
            xh[5 + q, rows, pl.ds(part * HALF, HALF)] = high
            xl[5 + q, rows, pl.ds(part * HALF, HALF)] = low

    def unfold_cols(p, rc):
        rows = pl.ds(p * HALF + rc, ROWS)
        for part in range(2):
            cols = pl.ds(part * HALF, HALF)
            even = fa[2, rows, cols]
            odd = fa[3, rows, cols]
            for h, value in enumerate((even + odd, even - odd)):
                high, low = split(value)
                xh[7 + p, pl.ds(part * HALF + rc, ROWS), pl.ds(h * HALF, HALF)] = high
                xl[7 + p, pl.ds(part * HALF + rc, ROWS), pl.ds(h * HALF, HALF)] = low

    part = functools.partial
    first = [part(sort_measured, p, h) for p in range(2) for h in range(2)]
    first = [part(left, fa, 0, 0, 0, 0)] + first[:2] + [part(left, fa, 1, 0, 1, 1)] + first[2:] + [select]
    first += [part(fold_cols, p, rc) for p in range(2) for rc in range(0, HALF, ROWS)]
    middle = [part(right, fb, 0, 1, 0, 3), part(right, fb, 1, 1, 1, 4)]
    middle += [part(misfit, q, rc) for q in range(2) for rc in range(0, SIDE, ROWS)]
    middle += [part(right, fa, 2, 0, 0, 5), part(right, fa, 3, 0, 1, 6)]
    middle += [part(unfold_cols, p, rc) for p in range(2) for rc in range(0, HALF, ROWS)]
    middle += [part(left, fb, 3, 1, 0, 7), part(left, fb, 4, 1, 1, 8)]
    return first, middle


def grad_steps(r, c, grad, probe, pgrad, patch, fb):
    j = c // HALF
    s = c % HALF
    lane = lax.broadcasted_iota(jnp.int32, (ROWS, HALF), 1)
    below_shift = lane < s

    def chunk(rc, t):
        rows = pl.ds(t * HALF + rc, ROWS)
        pieces = []
        for h in range(2):
            cols = pl.ds(h * HALF, HALF)
            er = fb[3, pl.ds(rc, ROWS), cols]
            ei = fb[3, pl.ds(HALF + rc, ROWS), cols]
            dr = fb[4, pl.ds(rc, ROWS), cols]
            di = fb[4, pl.ds(HALF + rc, ROWS), cols]
            br, bi = (er + dr, ei + di) if t == 0 else (er - dr, ei - di)
            qr = probe[0, rows, cols]
            qi = probe[1, rows, cols]
            pr = patch[0, h, rows, :]
            pi = patch[1, h, rows, :]
            pgrad[0, h, rows, :] += pr * br + pi * bi
            pgrad[1, h, rows, :] += pr * bi - pi * br
            pieces.append((qr * br + qi * bi, qr * bi - qi * br))
        target = pl.ds(r + t * HALF + rc, ROWS)
        for part in range(2):
            first = pltpu.roll(pieces[0][part], s, 1)
            second = pltpu.roll(pieces[1][part], s, 1)
            grad[part, j, target, :] += jnp.where(below_shift, 0.0, first)
            grad[part, j + 1, target, :] += jnp.where(below_shift, first, second)
            grad[part, j + 2, target, :] += jnp.where(below_shift, second, 0.0)

    return [functools.partial(chunk, rc, t) for rc in range(0, HALF, ROWS) for t in range(2)]


def interleaved(main, side):
    done = 0
    for i, step in enumerate(main):
        step()
        upto = (i + 1) * len(side) // len(main)
        for other in side[done:upto]:
            other()
        done = upto


def slots_kernel(plan, *refs):
    live, offsets, probe_in, pgrad_in, tab_in, sel_in, measured = refs[:7]
    n_in, n_out = len(plan["in"]), len(plan["out"])
    blocks = refs[7:7 + n_in]
    outs = refs[7 + n_in:7 + n_in + n_out]
    pgrad_out = refs[7 + n_in + n_out]
    pgrad, probe, tab, sel, ext, grad, meas, patch, xh, xl, fa, fb, order, sems, msems = refs[8 + n_in + n_out:]
    slots = measured.shape[0]

    early, late = [(probe_in, probe)], [(tab_in, tab), (sel_in, sel)]
    if plan["keep"]:
        pgrad[...] = jnp.zeros_like(pgrad)
    else:
        late.append((pgrad_in, pgrad))
    for (kind, panel, row, panels), block in zip(plan["in"], blocks):
        if kind == "grad":
            late.append((block, grad.at[:, pl.ds(panel, panels), pl.ds(row, block.shape[2]), :]))
            continue
        for part in range(2):
            first = block.shape[2] // HALF - panels
            for h in range(panels):
                early.append((
                    block.at[part, :, pl.ds((first + h) * HALF, HALF)],
                    ext.at[part, panel + h, pl.ds(row, block.shape[1]), :],
                ))
    loads = [pltpu.make_async_copy(*pair, sems.at[i]) for i, pair in enumerate(early + late)]
    for load in loads:
        load.start()
    for panel, panels, row, rows in plan["zero"]:
        grad[:, pl.ds(panel, panels), pl.ds(row, rows), :] = jnp.zeros((2, panels, rows, HALF), F32)

    def collect(g, n):
        order[n] = g
        r, c = offsets[0, g], offsets[1, g]
        inside = (r <= TILE - SIDE) & (c <= TILE - SIDE)
        used = (g < live[0]) & (inside if plan["keep"] else ~inside)
        return n + used.astype(jnp.int32)

    total = lax.fori_loop(0, slots, collect, jnp.int32(0))

    def fetch(n):
        slot = lax.rem(n, 2)
        return [
            pltpu.make_async_copy(measured.at[order[n], :, pl.ds(h * HALF, HALF)], meas.at[slot, h], msems.at[slot, h])
            for h in range(2)
        ]

    @pl.when(total > 0)
    def _():
        for copy in fetch(0):
            copy.start()

    for load in loads[:len(early)]:
        load.wait()

    def place(n):
        g = order[n]
        return offsets[0, g], offsets[1, g]

    @pl.when(total > 0)
    def _():
        fb[pl.ds(3, 2)] = jnp.zeros((2, SIDE, SIDE), F32)
        patch[2] = jnp.zeros((2, 2, SIDE, HALF), F32)
        r, c = place(0)
        for run in cut_steps(r, c, ext, probe, patch.at[0], xh, xl):
            run()
        for load in loads[len(early):]:
            load.wait()

        def step(n, carry):
            @pl.when(n + 1 < total)
            def _():
                for copy in fetch(n + 1):
                    copy.start()

            for copy in fetch(n):
                copy.wait()
            first, middle = transform_steps(meas.at[lax.rem(n, 2)], tab, sel, xh, xl, fa, fb)
            r, c = place(jnp.maximum(n - 1, 0))
            interleaved(
                first, grad_steps(r, c, grad, probe, pgrad, patch.at[lax.rem(n + 2, 3)], fb)
            )
            r, c = place(jnp.minimum(n + 1, total - 1))
            interleaved(middle, cut_steps(r, c, ext, probe, patch.at[lax.rem(n + 1, 3)], xh, xl))
            return carry

        lax.fori_loop(0, total, step, 0)
        r, c = place(total - 1)
        for run in grad_steps(r, c, grad, probe, pgrad, patch.at[lax.rem(total + 2, 3)], fb):
            run()

    @pl.when(total == 0)
    def _():
        for load in loads[len(early):]:
            load.wait()

    stores = [pltpu.make_async_copy(pgrad, pgrad_out, sems.at[0])]
    for (kind, panel, row, panels), out in zip(plan["out"], outs):
        if kind == "grad":
            pairs = [(grad.at[:, pl.ds(panel, panels), pl.ds(row, out.shape[2]), :], out)]
        else:
            pairs = []
            for part in range(2):
                first = out.shape[2] // HALF - panels
                for h in range(panels):
                    pairs.append((
                        grad.at[part, panel + h, pl.ds(row, out.shape[1]), :],
                        out.at[part, :, pl.ds((first + h) * HALF, HALF)],
                    ))
        for source, target in pairs:
            stores.append(pltpu.make_async_copy(source, target, sems.at[len(stores)]))
    for store in stores:
        store.start()
    for store in stores:
        store.wait()


PLAN_OWN = {
    "panels": 5, "keep": True,
    "in": [("ext", 0, 0, 4)],
    "zero": [(0, 4, 0, TILE)],
    "out": [("grad", 0, 0, 4)], "shapes": [(2, 4, TILE, HALF)],
}
PLAN_OUTER = {
    "panels": 6, "keep": False,
    "in": [("ext", 0, 0, 4), ("ext", 0, TILE, 4), ("ext", 4, 0, 2), ("ext", 4, TILE, 2), ("grad", 0, 0, 4)],
    "zero": [(0, 4, TILE, SIDE), (4, 2, 0, WIDE)],
    "out": [
        ("array", 4, TILE, 2), ("array", 4, 0, 2), ("array", 0, TILE, 2), ("array", 2, TILE, 2), ("array", 0, 0, 4),
    ],
    "shapes": [(2, SIDE, SIDE), (2, TILE, SIDE), (2, SIDE, SIDE), (2, SIDE, SIDE), (2, TILE, TILE)],
}


def slots_call(plan, live, offsets, probe, probe_grad, measured, blocks):
    tables, select = dft_tables()
    any_spec = pl.BlockSpec(memory_space=pl.ANY)
    smem = pl.BlockSpec(memory_space=pltpu.SMEM)
    shapes = plan["shapes"] + [(2, 2, SIDE, HALF)]
    rows, panels = WIDE, plan["panels"]
    return pl.pallas_call(
        functools.partial(slots_kernel, plan),
        out_shape=[jax.ShapeDtypeStruct(s, F32) for s in shapes],
        in_specs=[smem, smem] + [any_spec] * (5 + len(blocks)),
        out_specs=[any_spec] * len(shapes),
        scratch_shapes=[
            pltpu.VMEM((2, 2, SIDE, HALF), F32),
            pltpu.VMEM(probe.shape, F32),
            pltpu.VMEM(tables.shape, BF16),
            pltpu.VMEM(select.shape, BF16),
            pltpu.VMEM((2, panels, rows, HALF), F32),
            pltpu.VMEM((2, panels, rows, HALF), F32),
            pltpu.VMEM((2, 2, SIDE, HALF), F32),
            pltpu.VMEM((3, 2, 2, SIDE, HALF), F32),
            pltpu.VMEM((9, SIDE, SIDE), BF16),
            pltpu.VMEM((9, SIDE, SIDE), BF16),
            pltpu.VMEM((4, SIDE, SIDE), F32),
            pltpu.VMEM((5, SIDE, SIDE), F32),
            pltpu.SMEM((measured.shape[0],), jnp.int32),
            pltpu.SemaphoreType.DMA((32,)),
            pltpu.SemaphoreType.DMA((2, 2)),
        ],
        compiler_params=pltpu.CompilerParams(vmem_limit_bytes=56 * 1024 * 1024),
        cost_estimate=pl.CostEstimate(flops=2**20, bytes_accessed=2**20, transcendentals=0),
    )(live, offsets.T, probe, probe_grad, jnp.asarray(tables), jnp.asarray(select), measured, *blocks)


ROW_AXES = ("z", "y_lo", "core")
COL_AXES = ("x", "y_hi")
NEAR_AXES = ("z", "core", "x")
FAR_AXES = ("y_lo", "y_hi")


def passed_along(block, axes, distance):
    devices = range(lax.axis_size(axes))
    route = [(i - distance, i) for i in devices if i - distance in devices]
    return lax.ppermute(block, axes, route)


def passed_across(block, distance):
    rows, cols = lax.axis_size(ROW_AXES), lax.axis_size(COL_AXES)
    pairs = []
    for i in range(rows):
        for j in range(cols):
            if 0 <= i - distance < rows and 0 <= j - distance < cols:
                pairs.append(((i - distance) * cols + j - distance, i * cols + j))
    return lax.ppermute(block, ROW_AXES + COL_AXES, pairs)


def update_kernel(tile, own, from_left, above_left, above_right, across, out):
    top, low = pl.ds(0, SIDE), pl.ds(SIDE, TILE - SIDE)
    first, second = pl.ds(0, SIDE), pl.ds(SIDE, TILE - SIDE)
    for part in range(2):
        out[part, top, first] = tile[part, top, first] - 0.25 * (
            (own[part, top, first] + from_left[part, top, :]) + (above_left[part] + across[part])
        )
        out[part, low, first] = tile[part, low, first] - 0.25 * (own[part, low, first] + from_left[part, low, :])
        out[part, top, second] = tile[part, top, second] - 0.25 * (own[part, top, second] + above_right[part])
        out[part, low, second] = tile[part, low, second] - 0.25 * own[part, low, second]


def update(tile, *parts):
    return pl.pallas_call(
        update_kernel,
        out_shape=jax.ShapeDtypeStruct(tile.shape, F32),
        compiler_params=pltpu.CompilerParams(vmem_limit_bytes=32 * 1024 * 1024),
        cost_estimate=pl.CostEstimate(flops=2**20, bytes_accessed=2**20, transcendentals=0),
    )(tile, *parts)


def total_over_all(x):
    near = lax.axis_size(NEAR_AXES)
    blocks = x.reshape(-1, 8, HALF)
    shares = lax.all_to_all(blocks, NEAR_AXES, 0, 0, tiled=True)
    share = jnp.sum(shares.reshape(near, -1, 8, HALF), axis=0)
    far = lax.axis_size(FAR_AXES)
    others = [lax.ppermute(share, FAR_AXES, [(i, i ^ bits) for i in range(far)]) for bits in range(1, far)]
    share = (share + others[0]) + (others[1] + others[2])
    copies = jnp.broadcast_to(share[None], (near,) + share.shape).reshape(blocks.shape)
    return lax.all_to_all(copies, NEAR_AXES, 0, 0, tiled=True).reshape(x.shape)


def body(object_field, probe, measured, offsets, live):
    side = probe.shape[1]
    half = side // 2
    positions = measured.shape[0] * lax.axis_size(ROW_AXES) * lax.axis_size(COL_AXES)
    below = passed_along(object_field[:, :side, :], ROW_AXES, -1)
    right = passed_along(object_field[:, :, :side], COL_AXES, -1)
    corner = passed_across(object_field[:, :side, :side], -1)

    def call(plan, probe_grad, blocks):
        return slots_call(plan, live, offsets, probe, probe_grad, measured, blocks)

    grad_own, probe_grad = call(PLAN_OWN, jnp.zeros((2, 2, 8, half), F32), [object_field])
    below, right, corner, grad_own = lax.optimization_barrier((below, right, corner, grad_own))
    to_across, to_right, below_left, below_right, own_grad, probe_grad = call(
        PLAN_OUTER, probe_grad, [object_field, below, right, corner, grad_own]
    )
    from_left = passed_along(to_right, COL_AXES, 1)
    above_left = passed_along(below_left, ROW_AXES, 1)
    above_right = passed_along(below_right, ROW_AXES, 1)
    from_across = passed_across(to_across, 1)
    total_grad = total_over_all(probe_grad)
    object_next = update(object_field, own_grad, from_left, above_left, above_right, from_across)
    object_next, total_grad = lax.optimization_barrier((object_next, total_grad))
    total_grad = jnp.concatenate([total_grad[:, 0], total_grad[:, 1]], axis=2)
    probe_next = probe - (1.0 / math.sqrt(positions)) * total_grad
    return (object_next, probe_next)


def solution(mesh):
    whole = jax.sharding.Mesh(mesh.devices.reshape(4, 2, 2, 4, 2), ROW_AXES + COL_AXES)
    both = ROW_AXES + COL_AXES
    placed = (P(None, ROW_AXES, COL_AXES), P(), P(both, None), P(both), P(both))
    return jax.shard_map(
        body, mesh=whole, in_specs=placed, out_specs=(P(None, ROW_AXES, COL_AXES), P()), check_vma=False
    )
```

```python
import functools
import math

import jax
import jax.numpy as jnp
import ml_dtypes
import numpy as np
from jax import lax
from jax.experimental import pallas as pl
from jax.experimental.pallas import tpu as pltpu
from jax.sharding import PartitionSpec as P

BF16 = jnp.bfloat16
F32 = jnp.float32
SIDE = 256
HALF = 128
TILE = 512
WIDE = TILE + SIDE
ROWS = 64


def split_np(table):
    high = table.astype(ml_dtypes.bfloat16)
    low = (table - high.astype(np.float64)).astype(ml_dtypes.bfloat16)
    return high, low


def dft_tables():
    k = np.arange(HALF)[:, None]
    n = np.arange(HALF)[None, :]
    forward = []
    backward = []
    for parity in range(2):
        angle = -2.0 * math.pi * ((n * (2 * k + parity)) % SIDE) / SIDE
        cos = np.cos(angle) / math.sqrt(SIDE)
        sin = np.sin(angle) / math.sqrt(SIDE)
        stacked = np.block([[cos, -sin], [sin, cos]])
        forward.extend(split_np(stacked))
        backward.extend(split_np(stacked.T))
    tables = np.stack(forward + backward).reshape(2, 2, 2, SIDE, SIDE)
    order = np.concatenate([np.arange(0, SIDE, 2), np.arange(1, SIDE, 2)])
    select = np.zeros((SIDE, SIDE), np.float32)
    select[order, np.arange(SIDE)] = 1.0
    return tables, select.astype(ml_dtypes.bfloat16)


def split(x):
    high = x.astype(BF16)
    low = (x - high.astype(F32)).astype(BF16)
    return high, low


def mm(a, b):
    return lax.dot_general(a, b, (((1,), (0,)), ((), ())), preferred_element_type=F32)


def left3(high, low, x_high, x_low):
    return mm(high, x_high) + (mm(high, x_low) + mm(low, x_high))


def right3(x_high, x_low, high, low):
    return mm(x_high, high) + (mm(x_low, high) + mm(x_high, low))


def cut_steps(r, c, base, ext, probe, patch, xh, xl):
    j = c // HALF - base
    back_shift = lax.rem(HALF - c % HALF, HALF)
    lane = lax.broadcasted_iota(jnp.int32, (ROWS, HALF), 1)
    take_first = lane < HALF - c % HALF

    def chunk(rc):
        wave = []
        for t in range(2):
            cut = []
            rows = pl.ds(t * HALF + rc, ROWS)
            for part in range(2):
                rolled = [
                    pltpu.roll(ext[part, j + h, pl.ds(r + t * HALF + rc, ROWS), :], back_shift, 1) for h in range(3)
                ]
                halves = [jnp.where(take_first, rolled[h], rolled[h + 1]) for h in range(2)]
                for h in range(2):
                    patch[part, h, rows, :] = halves[h]
                cut.append(halves)
            here = []
            for h in range(2):
                cols = pl.ds(h * HALF, HALF)
                qr = probe[0, rows, cols]
                qi = probe[1, rows, cols]
                here.append((qr * cut[0][h] - qi * cut[1][h], qr * cut[1][h] + qi * cut[0][h]))
            wave.append(here)
        for h in range(2):
            for part in range(2):
                top = wave[0][h][part]
                bottom = wave[1][h][part]
                for p, folded in enumerate((top + bottom, top - bottom)):
                    high, low = split(folded)
                    xh[p, pl.ds(part * HALF + rc, ROWS), pl.ds(h * HALF, HALF)] = high
                    xl[p, pl.ds(part * HALF + rc, ROWS), pl.ds(h * HALF, HALF)] = low

    return [functools.partial(chunk, rc) for rc in range(0, HALF, ROWS)]


def transform_steps(meas, tab, sel, xh, xl, fa, fb):
    first, middle = [], []

    def left(out, k, table, p, source):
        out[k] = left3(tab[table, p, 0], tab[table, p, 1], xh[source], xl[source])

    def right(out, k, table, q, source):
        out[k] = right3(xh[source], xl[source], tab[table, q, 0], tab[table, q, 1])

    def sort_measured(p, h):
        high, low = split(meas[h, pl.ds(p, HALF, stride=2), :])
        xh[2, pl.ds(p * HALF, HALF), pl.ds(h * HALF, HALF)] = high
        xl[2, pl.ds(p * HALF, HALF), pl.ds(h * HALF, HALF)] = low

    def select():
        fb[2] = mm(xh[2], sel[...]) + mm(xl[2], sel[...])

    def fold_cols(p, rc):
        for part in range(2):
            rows = pl.ds(part * HALF + rc, ROWS)
            near = fa[p, rows, pl.ds(0, HALF)]
            far = fa[p, rows, pl.ds(HALF, HALF)]
            for q, folded in enumerate((near + far, near - far)):
                high, low = split(folded)
                xh[3 + q, pl.ds(p * HALF + rc, ROWS), pl.ds(part * HALF, HALF)] = high
                xl[3 + q, pl.ds(p * HALF + rc, ROWS), pl.ds(part * HALF, HALF)] = low

    def misfit(q, rc):
        rows = pl.ds(rc, ROWS)
        re = fb[q, rows, pl.ds(0, HALF)]
        im = fb[q, rows, pl.ds(HALF, HALF)]
        miss = re * re + im * im - fb[2, rows, pl.ds(q * HALF, HALF)]
        for part, value in enumerate((miss * re, miss * im)):
            high, low = split(value)
            xh[5 + q, rows, pl.ds(part * HALF, HALF)] = high
            xl[5 + q, rows, pl.ds(part * HALF, HALF)] = low

    def unfold_cols(p, rc):
        rows = pl.ds(p * HALF + rc, ROWS)
        for part in range(2):
            cols = pl.ds(part * HALF, HALF)
            even = fa[2, rows, cols]
            odd = fa[3, rows, cols]
            for h, value in enumerate((even + odd, even - odd)):
                high, low = split(value)
                xh[7 + p, pl.ds(part * HALF + rc, ROWS), pl.ds(h * HALF, HALF)] = high
                xl[7 + p, pl.ds(part * HALF + rc, ROWS), pl.ds(h * HALF, HALF)] = low

    part = functools.partial
    first = [part(sort_measured, p, h) for p in range(2) for h in range(2)]
    first = [part(left, fa, 0, 0, 0, 0)] + first[:2] + [part(left, fa, 1, 0, 1, 1)] + first[2:] + [select]
    first += [part(fold_cols, p, rc) for p in range(2) for rc in range(0, HALF, ROWS)]
    middle = [part(right, fb, 0, 1, 0, 3), part(right, fb, 1, 1, 1, 4)]
    middle += [part(misfit, q, rc) for q in range(2) for rc in range(0, SIDE, ROWS)]
    middle += [part(right, fa, 2, 0, 0, 5), part(right, fa, 3, 0, 1, 6)]
    middle += [part(unfold_cols, p, rc) for p in range(2) for rc in range(0, HALF, ROWS)]
    middle += [part(left, fb, 3, 1, 0, 7), part(left, fb, 4, 1, 1, 8)]
    return first, middle


def grad_steps(r, c, base, grad, probe, pgrad, patch, fb):
    j = c // HALF - base
    s = c % HALF
    lane = lax.broadcasted_iota(jnp.int32, (ROWS, HALF), 1)
    below_shift = lane < s

    def chunk(rc, t):
        rows = pl.ds(t * HALF + rc, ROWS)
        pieces = []
        for h in range(2):
            cols = pl.ds(h * HALF, HALF)
            er = fb[3, pl.ds(rc, ROWS), cols]
            ei = fb[3, pl.ds(HALF + rc, ROWS), cols]
            dr = fb[4, pl.ds(rc, ROWS), cols]
            di = fb[4, pl.ds(HALF + rc, ROWS), cols]
            br, bi = (er + dr, ei + di) if t == 0 else (er - dr, ei - di)
            qr = probe[0, rows, cols]
            qi = probe[1, rows, cols]
            pr = patch[0, h, rows, :]
            pi = patch[1, h, rows, :]
            pgrad[0, h, rows, :] += pr * br + pi * bi
            pgrad[1, h, rows, :] += pr * bi - pi * br
            pieces.append((qr * br + qi * bi, qr * bi - qi * br))
        target = pl.ds(r + t * HALF + rc, ROWS)
        for part in range(2):
            first = pltpu.roll(pieces[0][part], s, 1)
            second = pltpu.roll(pieces[1][part], s, 1)
            grad[part, j, target, :] += jnp.where(below_shift, 0.0, first)
            grad[part, j + 1, target, :] += jnp.where(below_shift, first, second)
            grad[part, j + 2, target, :] += jnp.where(below_shift, second, 0.0)

    return [functools.partial(chunk, rc, t) for rc in range(0, HALF, ROWS) for t in range(2)]


def interleaved(main, side):
    done = 0
    for i, step in enumerate(main):
        step()
        upto = (i + 1) * len(side) // len(main)
        for other in side[done:upto]:
            other()
        done = upto


def slots_kernel(plan, *refs):
    live, offsets, probe_in, pgrad_in, tab_in, sel_in, measured = refs[:7]
    n_in, n_out = len(plan["in"]), len(plan["out"])
    blocks = refs[7:7 + n_in]
    outs = refs[7 + n_in:7 + n_in + n_out]
    pgrad_out = refs[7 + n_in + n_out]
    pgrad, probe, tab, sel, ext, grad, meas, patch, xh, xl, fa, fb, order, sems, msems = refs[8 + n_in + n_out:]
    slots = measured.shape[0]

    early, late = [(probe_in, probe)], [(tab_in, tab), (sel_in, sel)]
    if plan["first"]:
        pgrad[...] = jnp.zeros_like(pgrad)
    else:
        late.append((pgrad_in, pgrad))
    for (kind, panel, row, panels, source, rows), block in zip(plan["in"], blocks):
        if kind == "grad":
            late.append((block, grad.at[:, pl.ds(panel, panels), pl.ds(row, block.shape[2]), :]))
            continue
        for part in range(2):
            first = block.shape[2] // HALF - panels
            for h in range(panels):
                early.append((
                    block.at[part, pl.ds(source, rows), pl.ds((first + h) * HALF, HALF)],
                    ext.at[part, panel + h, pl.ds(row, rows), :],
                ))
    loads = [pltpu.make_async_copy(*pair, sems.at[i]) for i, pair in enumerate(early + late)]
    for load in loads:
        load.start()
    for panel, panels, row, rows in plan["zero"]:
        grad[:, pl.ds(panel, panels), pl.ds(row, rows), :] = jnp.zeros((2, panels, rows, HALF), F32)

    def collect(g, n):
        order[n] = g
        r, c = offsets[0, g], offsets[1, g]
        low_r, high_r, low_c, high_c = plan["keep"]
        used = (g < live[0]) & (r >= low_r) & (r <= high_r) & (c >= low_c) & (c <= high_c)
        return n + used.astype(jnp.int32)

    total = lax.fori_loop(0, slots, collect, jnp.int32(0))

    def fetch(n):
        slot = lax.rem(n, 2)
        return [
            pltpu.make_async_copy(measured.at[order[n], :, pl.ds(h * HALF, HALF)], meas.at[slot, h], msems.at[slot, h])
            for h in range(2)
        ]

    @pl.when(total > 0)
    def _():
        for copy in fetch(0):
            copy.start()

    for load in loads[:len(early)]:
        load.wait()

    def place(n):
        g = order[n]
        return offsets[0, g], offsets[1, g]

    @pl.when(total > 0)
    def _():
        fb[pl.ds(3, 2)] = jnp.zeros((2, SIDE, SIDE), F32)
        patch[2] = jnp.zeros((2, 2, SIDE, HALF), F32)
        r, c = place(0)
        for run in cut_steps(r, c, plan["base"], ext, probe, patch.at[0], xh, xl):
            run()
        for load in loads[len(early):]:
            load.wait()

        def step(n, carry):
            @pl.when(n + 1 < total)
            def _():
                for copy in fetch(n + 1):
                    copy.start()

            for copy in fetch(n):
                copy.wait()
            first, middle = transform_steps(meas.at[lax.rem(n, 2)], tab, sel, xh, xl, fa, fb)
            r, c = place(jnp.maximum(n - 1, 0))
            interleaved(
                first, grad_steps(r, c, plan["base"], grad, probe, pgrad, patch.at[lax.rem(n + 2, 3)], fb)
            )
            r, c = place(jnp.minimum(n + 1, total - 1))
            interleaved(middle, cut_steps(r, c, plan["base"], ext, probe, patch.at[lax.rem(n + 1, 3)], xh, xl))
            return carry

        lax.fori_loop(0, total, step, 0)
        r, c = place(total - 1)
        for run in grad_steps(r, c, plan["base"], grad, probe, pgrad, patch.at[lax.rem(total + 2, 3)], fb):
            run()

    @pl.when(total == 0)
    def _():
        for load in loads[len(early):]:
            load.wait()

    stores = [pltpu.make_async_copy(pgrad, pgrad_out, sems.at[0])]
    for (kind, panel, row, panels), out in zip(plan["out"], outs):
        if kind == "grad":
            pairs = [(grad.at[:, pl.ds(panel, panels), pl.ds(row, out.shape[2]), :], out)]
        else:
            pairs = []
            for part in range(2):
                first = out.shape[2] // HALF - panels
                for h in range(panels):
                    pairs.append((
                        grad.at[part, panel + h, pl.ds(row, out.shape[1]), :],
                        out.at[part, :, pl.ds((first + h) * HALF, HALF)],
                    ))
        for source, target in pairs:
            stores.append(pltpu.make_async_copy(source, target, sems.at[len(stores)]))
    for store in stores:
        store.start()
    for store in stores:
        store.wait()


PLAN_OWN = {
    "base": 0, "panels": 5, "keep": (0, SIDE, 0, SIDE), "first": True,
    "in": [("ext", 0, 0, 4, 0, TILE)],
    "zero": [(0, 4, 0, TILE)],
    "out": [("array", 0, 0, 2), ("grad", 0, SIDE, 2), ("grad", 2, 0, 2)],
    "shapes": [(2, SIDE, SIDE), (2, 2, SIDE, HALF), (2, 2, TILE, HALF)],
}
PLAN_RIGHT = {
    "base": 2, "panels": 4, "keep": (0, SIDE, SIDE + 1, TILE), "first": False,
    "in": [("ext", 0, 0, 2, 0, TILE), ("ext", 2, 0, 2, 0, TILE), ("grad", 0, 0, 2, 0, TILE)],
    "zero": [(2, 2, 0, TILE)],
    "out": [("array", 0, 0, 2), ("array", 2, 0, 2), ("grad", 0, SIDE, 4)],
    "shapes": [(2, SIDE, SIDE), (2, SIDE, SIDE), (2, 4, SIDE, HALF)],
}
PLAN_LOWER = {
    "base": 0, "panels": 6, "keep": (SIDE + 1, TILE, 0, TILE), "first": False,
    "in": [
        ("ext", 0, SIDE, 4, SIDE, SIDE), ("ext", 0, TILE, 4, 0, SIDE), ("ext", 4, SIDE, 2, SIDE, SIDE),
        ("ext", 4, TILE, 2, 0, SIDE), ("grad", 0, SIDE, 2, 0, SIDE), ("grad", 2, SIDE, 4, 0, SIDE),
    ],
    "zero": [(0, 6, TILE, SIDE)],
    "out": [
        ("array", 4, TILE, 2), ("array", 4, SIDE, 2), ("array", 0, TILE, 2), ("array", 2, TILE, 2), ("array", 0, SIDE, 4),
    ],
    "shapes": [(2, SIDE, SIDE), (2, SIDE, SIDE), (2, SIDE, SIDE), (2, SIDE, SIDE), (2, SIDE, TILE)],
}


def slots_call(plan, live, offsets, probe, probe_grad, measured, blocks):
    tables, select = dft_tables()
    any_spec = pl.BlockSpec(memory_space=pl.ANY)
    smem = pl.BlockSpec(memory_space=pltpu.SMEM)
    shapes = plan["shapes"] + [(2, 2, SIDE, HALF)]
    rows, panels = WIDE, plan["panels"]
    return pl.pallas_call(
        functools.partial(slots_kernel, plan),
        out_shape=[jax.ShapeDtypeStruct(s, F32) for s in shapes],
        in_specs=[smem, smem] + [any_spec] * (5 + len(blocks)),
        out_specs=[any_spec] * len(shapes),
        scratch_shapes=[
            pltpu.VMEM((2, 2, SIDE, HALF), F32),
            pltpu.VMEM(probe.shape, F32),
            pltpu.VMEM(tables.shape, BF16),
            pltpu.VMEM(select.shape, BF16),
            pltpu.VMEM((2, panels, rows, HALF), F32),
            pltpu.VMEM((2, panels, rows, HALF), F32),
            pltpu.VMEM((2, 2, SIDE, HALF), F32),
            pltpu.VMEM((3, 2, 2, SIDE, HALF), F32),
            pltpu.VMEM((9, SIDE, SIDE), BF16),
            pltpu.VMEM((9, SIDE, SIDE), BF16),
            pltpu.VMEM((4, SIDE, SIDE), F32),
            pltpu.VMEM((5, SIDE, SIDE), F32),
            pltpu.SMEM((measured.shape[0],), jnp.int32),
            pltpu.SemaphoreType.DMA((32,)),
            pltpu.SemaphoreType.DMA((2, 2)),
        ],
        compiler_params=pltpu.CompilerParams(vmem_limit_bytes=56 * 1024 * 1024),
        cost_estimate=pl.CostEstimate(flops=2**20, bytes_accessed=2**20, transcendentals=0),
    )(live, offsets.T, probe, probe_grad, jnp.asarray(tables), jnp.asarray(select), measured, *blocks)


ROW_AXES = ("z", "y_lo", "core")
COL_AXES = ("x", "y_hi")
NEAR_AXES = ("z", "core", "x")
FAR_AXES = ("y_lo", "y_hi")


def passed_along(block, axes, distance):
    devices = range(lax.axis_size(axes))
    route = [(i - distance, i) for i in devices if i - distance in devices]
    return lax.ppermute(block, axes, route)


def passed_across(block, distance):
    rows, cols = lax.axis_size(ROW_AXES), lax.axis_size(COL_AXES)
    pairs = []
    for i in range(rows):
        for j in range(cols):
            if 0 <= i - distance < rows and 0 <= j - distance < cols:
                pairs.append(((i - distance) * cols + j - distance, i * cols + j))
    return lax.ppermute(block, ROW_AXES + COL_AXES, pairs)


def update_kernel(tile, top_left, top_right, lower, left_top, left_low, above_left, above_right, across, out):
    top, low = pl.ds(0, SIDE), pl.ds(SIDE, TILE - SIDE)
    first, second = pl.ds(0, SIDE), pl.ds(SIDE, TILE - SIDE)
    for part in range(2):
        out[part, top, first] = tile[part, top, first] - 0.25 * (
            (top_left[part] + left_top[part]) + (above_left[part] + across[part])
        )
        out[part, top, second] = tile[part, top, second] - 0.25 * (top_right[part] + above_right[part])
        out[part, low, first] = tile[part, low, first] - 0.25 * (lower[part, :, first] + left_low[part])
        out[part, low, second] = tile[part, low, second] - 0.25 * lower[part, :, second]


def update(tile, *parts):
    return pl.pallas_call(
        update_kernel,
        out_shape=jax.ShapeDtypeStruct(tile.shape, F32),
        compiler_params=pltpu.CompilerParams(vmem_limit_bytes=32 * 1024 * 1024),
        cost_estimate=pl.CostEstimate(flops=2**20, bytes_accessed=2**20, transcendentals=0),
    )(tile, *parts)


def probe_kernel(scale, probe, total, out):
    for part in range(2):
        for h in range(2):
            cols = pl.ds(h * HALF, HALF)
            out[part, :, cols] = probe[part, :, cols] - scale * total[part, h]


def probe_update(scale, probe, total):
    return pl.pallas_call(
        functools.partial(probe_kernel, scale),
        out_shape=jax.ShapeDtypeStruct(probe.shape, F32),
        cost_estimate=pl.CostEstimate(flops=2**20, bytes_accessed=2**20, transcendentals=0),
    )(probe, total)


def total_over_all(x, before):
    near = lax.axis_size(NEAR_AXES)
    blocks = x.reshape(-1, 8, HALF)
    shares = lax.all_to_all(blocks, NEAR_AXES, 0, 0, tiled=True)
    share = jnp.sum(shares.reshape(near, -1, 8, HALF), axis=0)
    far = lax.axis_size(FAR_AXES)
    copies = jnp.broadcast_to(share[None], (far,) + share.shape).reshape((-1,) + share.shape[1:])
    share = lax.all_to_all(copies, FAR_AXES, 0, 0, tiled=True)
    share = jnp.sum(share.reshape((far, -1) + share.shape[1:]), axis=0)
    share, before = lax.optimization_barrier((share, before))
    copies = jnp.broadcast_to(share[None], (near,) + share.shape).reshape(blocks.shape)
    return lax.all_to_all(copies, NEAR_AXES, 0, 0, tiled=True).reshape(x.shape), before


def body(object_field, probe, measured, offsets, live):
    side = probe.shape[1]
    half = side // 2
    positions = measured.shape[0] * lax.axis_size(ROW_AXES) * lax.axis_size(COL_AXES)
    right = passed_along(object_field[:, :, :side], COL_AXES, -1)

    def call(plan, probe_grad, blocks):
        return slots_call(plan, live, offsets, probe, probe_grad, measured, blocks)

    top_left, grad_left, grad_right, probe_grad = call(PLAN_OWN, jnp.zeros((2, 2, 8, half), F32), [object_field])
    below_source, corner_source, grad_right = lax.optimization_barrier(
        (object_field[:, :side, :], object_field[:, :side, :side], grad_right)
    )
    below = passed_along(below_source, ROW_AXES, -1)
    corner = passed_across(corner_source, -1)
    top_right, right_top, grad_low, probe_grad = call(PLAN_RIGHT, probe_grad, [object_field, right, grad_right])
    below, corner, grad_low, right_top = lax.optimization_barrier((below, corner, grad_low, right_top))
    left_top = passed_along(right_top, COL_AXES, 1)
    to_across, right_low, below_left, below_right, lower, probe_grad = call(
        PLAN_LOWER, probe_grad, [object_field, below, right, corner, grad_left, grad_low]
    )
    from_across = passed_across(to_across, 1)
    above_left = passed_along(below_left, ROW_AXES, 1)
    above_right = passed_along(below_right, ROW_AXES, 1)
    left_top, probe_grad = lax.optimization_barrier((left_top, probe_grad))
    total_grad, (from_across, right_low) = total_over_all(probe_grad, (from_across, right_low))
    left_low = passed_along(right_low, COL_AXES, 1)
    object_next = update(
        object_field, top_left, top_right, lower, left_top, left_low, above_left, above_right, from_across
    )
    object_next, total_grad = lax.optimization_barrier((object_next, total_grad))
    probe_next = probe_update(1.0 / math.sqrt(positions), probe, total_grad)
    return (object_next, probe_next)


def solution(mesh):
    whole = jax.sharding.Mesh(mesh.devices.reshape(4, 2, 2, 4, 2), ROW_AXES + COL_AXES)
    both = ROW_AXES + COL_AXES
    placed = (P(None, ROW_AXES, COL_AXES), P(), P(both, None), P(both), P(both))
    return jax.shard_map(
        body, mesh=whole, in_specs=placed, out_specs=(P(None, ROW_AXES, COL_AXES), P()), check_vma=False
    )
```

```python
import functools
import math

import jax
import jax.numpy as jnp
import ml_dtypes
import numpy as np
from jax import lax
from jax.experimental import pallas as pl
from jax.experimental.pallas import tpu as pltpu
from jax.sharding import PartitionSpec as P

BF16 = jnp.bfloat16
F32 = jnp.float32
SIDE = 256
HALF = 128
TILE = 512
WIDE = TILE + SIDE
ROWS = 64


def split_np(table):
    high = table.astype(ml_dtypes.bfloat16)
    low = (table - high.astype(np.float64)).astype(ml_dtypes.bfloat16)
    return high, low


def dft_tables():
    k = np.arange(HALF)[:, None]
    n = np.arange(HALF)[None, :]
    forward = []
    backward = []
    for parity in range(2):
        angle = -2.0 * math.pi * ((n * (2 * k + parity)) % SIDE) / SIDE
        cos = np.cos(angle) / math.sqrt(SIDE)
        sin = np.sin(angle) / math.sqrt(SIDE)
        stacked = np.block([[cos, -sin], [sin, cos]])
        forward.extend(split_np(stacked))
        backward.extend(split_np(stacked.T))
    tables = np.stack(forward + backward).reshape(2, 2, 2, SIDE, SIDE)
    order = np.concatenate([np.arange(0, SIDE, 2), np.arange(1, SIDE, 2)])
    select = np.zeros((SIDE, SIDE), np.float32)
    select[order, np.arange(SIDE)] = 1.0
    return tables, select.astype(ml_dtypes.bfloat16)


def split(x):
    high = x.astype(BF16)
    low = (x - high.astype(F32)).astype(BF16)
    return high, low


def mm(a, b):
    return lax.dot_general(a, b, (((1,), (0,)), ((), ())), preferred_element_type=F32)


def left3(high, low, x_high, x_low):
    return mm(high, x_high) + (mm(high, x_low) + mm(low, x_high))


def right3(x_high, x_low, high, low):
    return mm(x_high, high) + (mm(x_low, high) + mm(x_high, low))


def cut_steps(r, c, base, ext, probe, patch, xh, xl):
    j = c // HALF - base
    back_shift = lax.rem(HALF - c % HALF, HALF)
    lane = lax.broadcasted_iota(jnp.int32, (ROWS, HALF), 1)
    take_first = lane < HALF - c % HALF

    def chunk(rc):
        wave = []
        for t in range(2):
            cut = []
            rows = pl.ds(t * HALF + rc, ROWS)
            for part in range(2):
                rolled = [
                    pltpu.roll(ext[part, j + h, pl.ds(r + t * HALF + rc, ROWS), :], back_shift, 1) for h in range(3)
                ]
                halves = [jnp.where(take_first, rolled[h], rolled[h + 1]) for h in range(2)]
                for h in range(2):
                    patch[part, h, rows, :] = halves[h]
                cut.append(halves)
            here = []
            for h in range(2):
                cols = pl.ds(h * HALF, HALF)
                qr = probe[0, rows, cols]
                qi = probe[1, rows, cols]
                here.append((qr * cut[0][h] - qi * cut[1][h], qr * cut[1][h] + qi * cut[0][h]))
            wave.append(here)
        for h in range(2):
            for part in range(2):
                top = wave[0][h][part]
                bottom = wave[1][h][part]
                for p, folded in enumerate((top + bottom, top - bottom)):
                    high, low = split(folded)
                    xh[p, pl.ds(part * HALF + rc, ROWS), pl.ds(h * HALF, HALF)] = high
                    xl[p, pl.ds(part * HALF + rc, ROWS), pl.ds(h * HALF, HALF)] = low

    return [functools.partial(chunk, rc) for rc in range(0, HALF, ROWS)]


def transform_steps(meas, tab, sel, xh, xl, fa, fb):
    first, middle = [], []

    def left(out, k, table, p, source):
        out[k] = left3(tab[table, p, 0], tab[table, p, 1], xh[source], xl[source])

    def right(out, k, table, q, source):
        out[k] = right3(xh[source], xl[source], tab[table, q, 0], tab[table, q, 1])

    def sort_measured(p, h):
        high, low = split(meas[h, pl.ds(p, HALF, stride=2), :])
        xh[2, pl.ds(p * HALF, HALF), pl.ds(h * HALF, HALF)] = high
        xl[2, pl.ds(p * HALF, HALF), pl.ds(h * HALF, HALF)] = low

    def select():
        fb[2] = mm(xh[2], sel[...]) + mm(xl[2], sel[...])

    def fold_cols(p, rc):
        for part in range(2):
            rows = pl.ds(part * HALF + rc, ROWS)
            near = fa[p, rows, pl.ds(0, HALF)]
            far = fa[p, rows, pl.ds(HALF, HALF)]
            for q, folded in enumerate((near + far, near - far)):
                high, low = split(folded)
                xh[3 + q, pl.ds(p * HALF + rc, ROWS), pl.ds(part * HALF, HALF)] = high
                xl[3 + q, pl.ds(p * HALF + rc, ROWS), pl.ds(part * HALF, HALF)] = low

    def misfit(q, rc):
        rows = pl.ds(rc, ROWS)
        re = fb[q, rows, pl.ds(0, HALF)]
        im = fb[q, rows, pl.ds(HALF, HALF)]
        miss = re * re + im * im - fb[2, rows, pl.ds(q * HALF, HALF)]
        for part, value in enumerate((miss * re, miss * im)):
            high, low = split(value)
            xh[5 + q, rows, pl.ds(part * HALF, HALF)] = high
            xl[5 + q, rows, pl.ds(part * HALF, HALF)] = low

    def unfold_cols(p, rc):
        rows = pl.ds(p * HALF + rc, ROWS)
        for part in range(2):
            cols = pl.ds(part * HALF, HALF)
            even = fa[2, rows, cols]
            odd = fa[3, rows, cols]
            for h, value in enumerate((even + odd, even - odd)):
                high, low = split(value)
                xh[7 + p, pl.ds(part * HALF + rc, ROWS), pl.ds(h * HALF, HALF)] = high
                xl[7 + p, pl.ds(part * HALF + rc, ROWS), pl.ds(h * HALF, HALF)] = low

    part = functools.partial
    first = [part(sort_measured, p, h) for p in range(2) for h in range(2)]
    first = [part(left, fa, 0, 0, 0, 0)] + first[:2] + [part(left, fa, 1, 0, 1, 1)] + first[2:] + [select]
    first += [part(fold_cols, p, rc) for p in range(2) for rc in range(0, HALF, ROWS)]
    middle = [part(right, fb, 0, 1, 0, 3), part(right, fb, 1, 1, 1, 4)]
    middle += [part(misfit, q, rc) for q in range(2) for rc in range(0, SIDE, ROWS)]
    middle += [part(right, fa, 2, 0, 0, 5), part(right, fa, 3, 0, 1, 6)]
    middle += [part(unfold_cols, p, rc) for p in range(2) for rc in range(0, HALF, ROWS)]
    middle += [part(left, fb, 3, 1, 0, 7), part(left, fb, 4, 1, 1, 8)]
    return first, middle


def grad_steps(r, c, base, grad, probe, pgrad, patch, fb):
    j = c // HALF - base
    s = c % HALF
    lane = lax.broadcasted_iota(jnp.int32, (ROWS, HALF), 1)
    below_shift = lane < s

    def chunk(rc, t):
        rows = pl.ds(t * HALF + rc, ROWS)
        pieces = []
        for h in range(2):
            cols = pl.ds(h * HALF, HALF)
            er = fb[3, pl.ds(rc, ROWS), cols]
            ei = fb[3, pl.ds(HALF + rc, ROWS), cols]
            dr = fb[4, pl.ds(rc, ROWS), cols]
            di = fb[4, pl.ds(HALF + rc, ROWS), cols]
            br, bi = (er + dr, ei + di) if t == 0 else (er - dr, ei - di)
            qr = probe[0, rows, cols]
            qi = probe[1, rows, cols]
            pr = patch[0, h, rows, :]
            pi = patch[1, h, rows, :]
            pgrad[0, h, rows, :] += pr * br + pi * bi
            pgrad[1, h, rows, :] += pr * bi - pi * br
            pieces.append((qr * br + qi * bi, qr * bi - qi * br))
        target = pl.ds(r + t * HALF + rc, ROWS)
        for part in range(2):
            first = pltpu.roll(pieces[0][part], s, 1)
            second = pltpu.roll(pieces[1][part], s, 1)
            grad[part, j, target, :] += jnp.where(below_shift, 0.0, first)
            grad[part, j + 1, target, :] += jnp.where(below_shift, first, second)
            grad[part, j + 2, target, :] += jnp.where(below_shift, second, 0.0)

    return [functools.partial(chunk, rc, t) for rc in range(0, HALF, ROWS) for t in range(2)]


def interleaved(main, side):
    done = 0
    for i, step in enumerate(main):
        step()
        upto = (i + 1) * len(side) // len(main)
        for other in side[done:upto]:
            other()
        done = upto


def slots_kernel(plan, *refs):
    live, offsets, probe_in, pgrad_in, tab_in, sel_in, measured = refs[:7]
    n_in, n_out = len(plan["in"]), len(plan["out"])
    blocks = refs[7:7 + n_in]
    outs = refs[7 + n_in:7 + n_in + n_out]
    pgrad_out = refs[7 + n_in + n_out]
    pgrad, probe, tab, sel, ext, grad, meas, patch, xh, xl, fa, fb, order, sems, msems = refs[8 + n_in + n_out:]
    slots = measured.shape[0]

    early, late = [(probe_in, probe)], [(tab_in, tab), (sel_in, sel)]
    if plan["first"]:
        pgrad[...] = jnp.zeros_like(pgrad)
    else:
        late.append((pgrad_in, pgrad))
    for (kind, panel, row, panels, source, rows), block in zip(plan["in"], blocks):
        if kind == "grad":
            late.append((block, grad.at[:, pl.ds(panel, panels), pl.ds(row, block.shape[2]), :]))
            continue
        for part in range(2):
            first = block.shape[2] // HALF - panels
            for h in range(panels):
                early.append((
                    block.at[part, pl.ds(source, rows), pl.ds((first + h) * HALF, HALF)],
                    ext.at[part, panel + h, pl.ds(row, rows), :],
                ))
    loads = [pltpu.make_async_copy(*pair, sems.at[i]) for i, pair in enumerate(early + late)]
    for load in loads:
        load.start()
    for panel, panels, row, rows in plan["zero"]:
        grad[:, pl.ds(panel, panels), pl.ds(row, rows), :] = jnp.zeros((2, panels, rows, HALF), F32)

    def collect(g, n):
        order[n] = g
        r, c = offsets[0, g], offsets[1, g]
        low_r, high_r, low_c, high_c = plan["keep"]
        used = (g < live[0]) & (r >= low_r) & (r <= high_r) & (c >= low_c) & (c <= high_c)
        return n + used.astype(jnp.int32)

    total = lax.fori_loop(0, slots, collect, jnp.int32(0))

    def fetch(n):
        slot = lax.rem(n, 2)
        return [
            pltpu.make_async_copy(measured.at[order[n], :, pl.ds(h * HALF, HALF)], meas.at[slot, h], msems.at[slot, h])
            for h in range(2)
        ]

    @pl.when(total > 0)
    def _():
        for copy in fetch(0):
            copy.start()

    for load in loads[:len(early)]:
        load.wait()

    def place(n):
        g = order[n]
        return offsets[0, g], offsets[1, g]

    @pl.when(total > 0)
    def _():
        fb[pl.ds(3, 2)] = jnp.zeros((2, SIDE, SIDE), F32)
        patch[2] = jnp.zeros((2, 2, SIDE, HALF), F32)
        r, c = place(0)
        for run in cut_steps(r, c, plan["base"], ext, probe, patch.at[0], xh, xl):
            run()
        for load in loads[len(early):]:
            load.wait()

        def step(n, carry):
            @pl.when(n + 1 < total)
            def _():
                for copy in fetch(n + 1):
                    copy.start()

            for copy in fetch(n):
                copy.wait()
            first, middle = transform_steps(meas.at[lax.rem(n, 2)], tab, sel, xh, xl, fa, fb)
            r, c = place(jnp.maximum(n - 1, 0))
            interleaved(
                first, grad_steps(r, c, plan["base"], grad, probe, pgrad, patch.at[lax.rem(n + 2, 3)], fb)
            )
            r, c = place(jnp.minimum(n + 1, total - 1))
            interleaved(middle, cut_steps(r, c, plan["base"], ext, probe, patch.at[lax.rem(n + 1, 3)], xh, xl))
            return carry

        lax.fori_loop(0, total, step, 0)
        r, c = place(total - 1)
        for run in grad_steps(r, c, plan["base"], grad, probe, pgrad, patch.at[lax.rem(total + 2, 3)], fb):
            run()

    @pl.when(total == 0)
    def _():
        for load in loads[len(early):]:
            load.wait()

    stores = [pltpu.make_async_copy(pgrad, pgrad_out, sems.at[0])]
    for (kind, panel, row, panels), out in zip(plan["out"], outs):
        if kind == "grad":
            pairs = [(grad.at[:, pl.ds(panel, panels), pl.ds(row, out.shape[2]), :], out)]
        else:
            here = pl.ds(panel, panels), pl.ds(row, out.shape[1])
            if kind == "tile":
                grad[:, *here, :] = ext[:, *here, :] - 0.25 * grad[:, *here, :]
            pairs = []
            for part in range(2):
                first = out.shape[2] // HALF - panels
                for h in range(panels):
                    pairs.append((
                        grad.at[part, panel + h, pl.ds(row, out.shape[1]), :],
                        out.at[part, :, pl.ds((first + h) * HALF, HALF)],
                    ))
        for source, target in pairs:
            stores.append(pltpu.make_async_copy(source, target, sems.at[len(stores)]))
    for store in stores:
        store.start()
    for store in stores:
        store.wait()


PLAN_OWN = {
    "base": 0, "panels": 5, "keep": (0, SIDE, 0, SIDE), "first": True,
    "in": [("ext", 0, 0, 4, 0, TILE)],
    "zero": [(0, 4, 0, TILE)],
    "out": [("tile", 0, 0, 2), ("grad", 0, SIDE, 2), ("grad", 2, 0, 2)],
    "shapes": [(2, SIDE, SIDE), (2, 2, SIDE, HALF), (2, 2, TILE, HALF)],
}
PLAN_RIGHT = {
    "base": 2, "panels": 4, "keep": (0, SIDE, SIDE + 1, TILE), "first": False,
    "in": [("ext", 0, 0, 2, 0, TILE), ("ext", 2, 0, 2, 0, TILE), ("grad", 0, 0, 2, 0, TILE)],
    "zero": [(2, 2, 0, TILE)],
    "out": [("tile", 0, 0, 2), ("array", 2, 0, 2), ("grad", 0, SIDE, 4)],
    "shapes": [(2, SIDE, SIDE), (2, SIDE, SIDE), (2, 4, SIDE, HALF)],
}
PLAN_LOWER = {
    "base": 0, "panels": 6, "keep": (SIDE + 1, TILE, 0, TILE), "first": False,
    "in": [
        ("ext", 0, SIDE, 4, SIDE, SIDE), ("ext", 0, TILE, 4, 0, SIDE), ("ext", 4, SIDE, 2, SIDE, SIDE),
        ("ext", 4, TILE, 2, 0, SIDE), ("grad", 0, SIDE, 2, 0, SIDE), ("grad", 2, SIDE, 4, 0, SIDE),
    ],
    "zero": [(0, 6, TILE, SIDE)],
    "out": [
        ("array", 4, TILE, 2), ("array", 4, SIDE, 2), ("array", 0, TILE, 2), ("array", 2, TILE, 2), ("tile", 0, SIDE, 4),
    ],
    "shapes": [(2, SIDE, SIDE), (2, SIDE, SIDE), (2, SIDE, SIDE), (2, SIDE, SIDE), (2, SIDE, TILE)],
}


def slots_call(plan, live, offsets, probe, probe_grad, measured, blocks):
    tables, select = dft_tables()
    any_spec = pl.BlockSpec(memory_space=pl.ANY)
    smem = pl.BlockSpec(memory_space=pltpu.SMEM)
    shapes = plan["shapes"] + [(2, 2, SIDE, HALF)]
    rows, panels = WIDE, plan["panels"]
    return pl.pallas_call(
        functools.partial(slots_kernel, plan),
        out_shape=[jax.ShapeDtypeStruct(s, F32) for s in shapes],
        in_specs=[smem, smem] + [any_spec] * (5 + len(blocks)),
        out_specs=[any_spec] * len(shapes),
        scratch_shapes=[
            pltpu.VMEM((2, 2, SIDE, HALF), F32),
            pltpu.VMEM(probe.shape, F32),
            pltpu.VMEM(tables.shape, BF16),
            pltpu.VMEM(select.shape, BF16),
            pltpu.VMEM((2, panels, rows, HALF), F32),
            pltpu.VMEM((2, panels, rows, HALF), F32),
            pltpu.VMEM((2, 2, SIDE, HALF), F32),
            pltpu.VMEM((3, 2, 2, SIDE, HALF), F32),
            pltpu.VMEM((9, SIDE, SIDE), BF16),
            pltpu.VMEM((9, SIDE, SIDE), BF16),
            pltpu.VMEM((4, SIDE, SIDE), F32),
            pltpu.VMEM((5, SIDE, SIDE), F32),
            pltpu.SMEM((measured.shape[0],), jnp.int32),
            pltpu.SemaphoreType.DMA((32,)),
            pltpu.SemaphoreType.DMA((2, 2)),
        ],
        compiler_params=pltpu.CompilerParams(vmem_limit_bytes=56 * 1024 * 1024),
        cost_estimate=pl.CostEstimate(flops=2**20, bytes_accessed=2**20, transcendentals=0),
    )(live, offsets.T, probe, probe_grad, jnp.asarray(tables), jnp.asarray(select), measured, *blocks)


ROW_AXES = ("z", "y_lo", "core")
COL_AXES = ("x", "y_hi")
NEAR_AXES = ("z", "core", "x")
FAR_AXES = ("y_lo", "y_hi")


def passed_along(block, axes, distance):
    devices = range(lax.axis_size(axes))
    route = [(i - distance, i) for i in devices if i - distance in devices]
    return lax.ppermute(block, axes, route)


def passed_across(block, distance):
    rows, cols = lax.axis_size(ROW_AXES), lax.axis_size(COL_AXES)
    pairs = []
    for i in range(rows):
        for j in range(cols):
            if 0 <= i - distance < rows and 0 <= j - distance < cols:
                pairs.append(((i - distance) * cols + j - distance, i * cols + j))
    return lax.ppermute(block, ROW_AXES + COL_AXES, pairs)


def copied(pairs, sems):
    copies = [pltpu.make_async_copy(*pair, sems.at[i]) for i, pair in enumerate(pairs)]
    for copy in copies:
        copy.start()
    for copy in copies:
        copy.wait()


def top_kernel(
    top_left, top_right, lower, left_top, above_left, above_right, across, out,
    tile_v, left_v, above_v, across_v, sems,
):
    top, low = pl.ds(0, SIDE), pl.ds(SIDE, TILE - SIDE)
    first, second = pl.ds(0, SIDE), pl.ds(SIDE, TILE - SIDE)
    copied([
        (top_left, tile_v.at[:, top, first]), (top_right, tile_v.at[:, top, second]), (lower, tile_v.at[:, low, :]),
        (above_left, above_v.at[0]), (above_right, above_v.at[1]), (across, across_v), (left_top, left_v),
    ], sems)
    for part in range(2):
        tile_v[part, top, first] -= 0.25 * (left_v[part] + (above_v[0, part] + across_v[part]))
        tile_v[part, top, second] -= 0.25 * above_v[1, part]
    copied([(tile_v.at[part], out.at[part]) for part in range(2)], sems)


def low_kernel(scale, tile, left_low, probe, total, out, probe_out, tile_v, left_v, probe_v, total_v, sems):
    corner = pl.ds(0, 2), pl.ds(SIDE, TILE - SIDE), pl.ds(0, SIDE)
    copied([(tile.at[corner], tile_v), (left_low, left_v), (probe, probe_v), (total, total_v)], sems)
    tile_v[...] -= 0.25 * left_v[...]
    for part in range(2):
        for h in range(2):
            cols = pl.ds(h * HALF, HALF)
            probe_v[part, :, cols] -= scale * total_v[part, h]
    copied([(tile_v, out.at[corner]), (probe_v, probe_out)], sems)


def update_top(*parts):
    any_spec = pl.BlockSpec(memory_space=pl.ANY)
    return pl.pallas_call(
        top_kernel,
        out_shape=jax.ShapeDtypeStruct((2, TILE, TILE), F32),
        in_specs=[any_spec] * len(parts),
        out_specs=any_spec,
        scratch_shapes=[
            pltpu.VMEM((2, TILE, TILE), F32),
            pltpu.VMEM((2, SIDE, SIDE), F32),
            pltpu.VMEM((2, 2, SIDE, SIDE), F32),
            pltpu.VMEM((2, SIDE, SIDE), F32),
            pltpu.SemaphoreType.DMA((7,)),
        ],
        compiler_params=pltpu.CompilerParams(vmem_limit_bytes=56 * 1024 * 1024),
        cost_estimate=pl.CostEstimate(flops=2**20, bytes_accessed=2**20, transcendentals=0),
    )(*parts)


def update_low(scale, *parts):
    any_spec = pl.BlockSpec(memory_space=pl.ANY)
    tile, left_low, probe, total = parts
    return pl.pallas_call(
        functools.partial(low_kernel, scale),
        out_shape=[jax.ShapeDtypeStruct(tile.shape, F32), jax.ShapeDtypeStruct(probe.shape, F32)],
        in_specs=[any_spec] * len(parts),
        out_specs=[any_spec] * 2,
        scratch_shapes=[
            pltpu.VMEM(left_low.shape, F32),
            pltpu.VMEM(left_low.shape, F32),
            pltpu.VMEM(probe.shape, F32),
            pltpu.VMEM(total.shape, F32),
            pltpu.SemaphoreType.DMA((4,)),
        ],
        input_output_aliases={0: 0},
        compiler_params=pltpu.CompilerParams(vmem_limit_bytes=56 * 1024 * 1024),
        cost_estimate=pl.CostEstimate(flops=2**20, bytes_accessed=2**20, transcendentals=0),
    )(*parts)


def total_over_all(x, before):
    near = lax.axis_size(NEAR_AXES)
    blocks = x.reshape(-1, 8, HALF)
    shares = lax.all_to_all(blocks, NEAR_AXES, 0, 0, tiled=True)
    share = jnp.sum(shares.reshape(near, -1, 8, HALF), axis=0)
    far = lax.axis_size(FAR_AXES)
    copies = jnp.broadcast_to(share[None], (far,) + share.shape).reshape((-1,) + share.shape[1:])
    share = lax.all_to_all(copies, FAR_AXES, 0, 0, tiled=True)
    share = jnp.sum(share.reshape((far, -1) + share.shape[1:]), axis=0)
    share, before = lax.optimization_barrier((share, before))
    copies = jnp.broadcast_to(share[None], (near,) + share.shape).reshape(blocks.shape)
    return lax.all_to_all(copies, NEAR_AXES, 0, 0, tiled=True).reshape(x.shape), before


def body(object_field, probe, measured, offsets, live):
    side = probe.shape[1]
    half = side // 2
    positions = measured.shape[0] * lax.axis_size(ROW_AXES) * lax.axis_size(COL_AXES)
    right = passed_along(object_field[:, :, :side], COL_AXES, -1)

    def call(plan, probe_grad, blocks):
        return slots_call(plan, live, offsets, probe, probe_grad, measured, blocks)

    top_left, grad_left, grad_right, probe_grad = call(PLAN_OWN, jnp.zeros((2, 2, 8, half), F32), [object_field])
    below_source, corner_source, grad_right = lax.optimization_barrier(
        (object_field[:, :side, :], object_field[:, :side, :side], grad_right)
    )
    below = passed_along(below_source, ROW_AXES, -1)
    corner = passed_across(corner_source, -1)
    top_right, right_top, grad_low, probe_grad = call(PLAN_RIGHT, probe_grad, [object_field, right, grad_right])
    below, corner, grad_low, right_top = lax.optimization_barrier((below, corner, grad_low, right_top))
    left_top = passed_along(right_top, COL_AXES, 1)
    to_across, right_low, below_left, below_right, lower, probe_grad = call(
        PLAN_LOWER, probe_grad, [object_field, below, right, corner, grad_left, grad_low]
    )
    from_across = passed_across(to_across, 1)
    above_left = passed_along(below_left, ROW_AXES, 1)
    above_right = passed_along(below_right, ROW_AXES, 1)
    left_top, probe_grad = lax.optimization_barrier((left_top, probe_grad))
    total_grad, (from_across, above_left, right_low) = total_over_all(probe_grad, (from_across, above_left, right_low))
    left_low = passed_along(right_low, COL_AXES, 1)
    tile = update_top(top_left, top_right, lower, left_top, above_left, above_right, from_across)
    object_next, probe_next = update_low(1.0 / math.sqrt(positions), tile, left_low, probe, total_grad)
    return (object_next, probe_next)


def solution(mesh):
    whole = jax.sharding.Mesh(mesh.devices.reshape(4, 2, 2, 4, 2), ROW_AXES + COL_AXES)
    both = ROW_AXES + COL_AXES
    placed = (P(None, ROW_AXES, COL_AXES), P(), P(both, None), P(both), P(both))
    return jax.shard_map(
        body, mesh=whole, in_specs=placed, out_specs=(P(None, ROW_AXES, COL_AXES), P()), check_vma=False
    )
```

```python
import functools
import math

import jax
import jax.numpy as jnp
import ml_dtypes
import numpy as np
from jax import lax
from jax.experimental import pallas as pl
from jax.experimental.pallas import tpu as pltpu
from jax.sharding import PartitionSpec as P

BF16 = jnp.bfloat16
F32 = jnp.float32
SIDE = 256
HALF = 128
TILE = 512
WIDE = TILE + SIDE
ROWS = 64


def split_np(table):
    high = table.astype(ml_dtypes.bfloat16)
    low = (table - high.astype(np.float64)).astype(ml_dtypes.bfloat16)
    return high, low


def dft_tables():
    k = np.arange(HALF)[:, None]
    n = np.arange(HALF)[None, :]
    forward = []
    backward = []
    for parity in range(2):
        angle = -2.0 * math.pi * ((n * (2 * k + parity)) % SIDE) / SIDE
        cos = np.cos(angle) / math.sqrt(SIDE)
        sin = np.sin(angle) / math.sqrt(SIDE)
        stacked = np.block([[cos, -sin], [sin, cos]])
        forward.extend(split_np(stacked))
        backward.extend(split_np(stacked.T))
    tables = np.stack(forward + backward).reshape(2, 2, 2, SIDE, SIDE)
    order = np.concatenate([np.arange(0, SIDE, 2), np.arange(1, SIDE, 2)])
    select = np.zeros((SIDE, SIDE), np.float32)
    select[order, np.arange(SIDE)] = 1.0
    return tables, select.astype(ml_dtypes.bfloat16)


def split(x):
    high = x.astype(BF16)
    low = (x - high.astype(F32)).astype(BF16)
    return high, low


def mm(a, b):
    return lax.dot_general(a, b, (((1,), (0,)), ((), ())), preferred_element_type=F32)


def left3(high, low, x_high, x_low):
    return mm(high, x_high) + (mm(high, x_low) + mm(low, x_high))


def right3(x_high, x_low, high, low):
    return mm(x_high, high) + (mm(x_low, high) + mm(x_high, low))


def cut_steps(r, c, base, ext, probe, patch, xh, xl):
    j = c // HALF - base
    back_shift = lax.rem(HALF - c % HALF, HALF)
    lane = lax.broadcasted_iota(jnp.int32, (ROWS, HALF), 1)
    take_first = lane < HALF - c % HALF

    def chunk(rc):
        wave = []
        for t in range(2):
            cut = []
            rows = pl.ds(t * HALF + rc, ROWS)
            for part in range(2):
                rolled = [
                    pltpu.roll(ext[part, j + h, pl.ds(r + t * HALF + rc, ROWS), :], back_shift, 1) for h in range(3)
                ]
                halves = [jnp.where(take_first, rolled[h], rolled[h + 1]) for h in range(2)]
                for h in range(2):
                    patch[part, h, rows, :] = halves[h]
                cut.append(halves)
            here = []
            for h in range(2):
                cols = pl.ds(h * HALF, HALF)
                qr = probe[0, rows, cols]
                qi = probe[1, rows, cols]
                here.append((qr * cut[0][h] - qi * cut[1][h], qr * cut[1][h] + qi * cut[0][h]))
            wave.append(here)
        for h in range(2):
            for part in range(2):
                top = wave[0][h][part]
                bottom = wave[1][h][part]
                for p, folded in enumerate((top + bottom, top - bottom)):
                    high, low = split(folded)
                    xh[p, pl.ds(part * HALF + rc, ROWS), pl.ds(h * HALF, HALF)] = high
                    xl[p, pl.ds(part * HALF + rc, ROWS), pl.ds(h * HALF, HALF)] = low

    return [functools.partial(chunk, rc) for rc in range(0, HALF, ROWS)]


def transform_steps(meas, tab, sel, xh, xl, fa, fb):
    first, middle = [], []

    def left(out, k, table, p, source):
        out[k] = left3(tab[table, p, 0], tab[table, p, 1], xh[source], xl[source])

    def right(out, k, table, q, source):
        out[k] = right3(xh[source], xl[source], tab[table, q, 0], tab[table, q, 1])

    def sort_measured(p, h):
        high, low = split(meas[h, pl.ds(p, HALF, stride=2), :])
        xh[2, pl.ds(p * HALF, HALF), pl.ds(h * HALF, HALF)] = high
        xl[2, pl.ds(p * HALF, HALF), pl.ds(h * HALF, HALF)] = low

    def select():
        fb[2] = mm(xh[2], sel[...]) + mm(xl[2], sel[...])

    def fold_cols(p, rc):
        for part in range(2):
            rows = pl.ds(part * HALF + rc, ROWS)
            near = fa[p, rows, pl.ds(0, HALF)]
            far = fa[p, rows, pl.ds(HALF, HALF)]
            for q, folded in enumerate((near + far, near - far)):
                high, low = split(folded)
                xh[3 + q, pl.ds(p * HALF + rc, ROWS), pl.ds(part * HALF, HALF)] = high
                xl[3 + q, pl.ds(p * HALF + rc, ROWS), pl.ds(part * HALF, HALF)] = low

    def misfit(q, rc):
        rows = pl.ds(rc, ROWS)
        re = fb[q, rows, pl.ds(0, HALF)]
        im = fb[q, rows, pl.ds(HALF, HALF)]
        miss = re * re + im * im - fb[2, rows, pl.ds(q * HALF, HALF)]
        for part, value in enumerate((miss * re, miss * im)):
            high, low = split(value)
            xh[5 + q, rows, pl.ds(part * HALF, HALF)] = high
            xl[5 + q, rows, pl.ds(part * HALF, HALF)] = low

    def unfold_cols(p, rc):
        rows = pl.ds(p * HALF + rc, ROWS)
        for part in range(2):
            cols = pl.ds(part * HALF, HALF)
            even = fa[2, rows, cols]
            odd = fa[3, rows, cols]
            for h, value in enumerate((even + odd, even - odd)):
                high, low = split(value)
                xh[7 + p, pl.ds(part * HALF + rc, ROWS), pl.ds(h * HALF, HALF)] = high
                xl[7 + p, pl.ds(part * HALF + rc, ROWS), pl.ds(h * HALF, HALF)] = low

    part = functools.partial
    first = [part(sort_measured, p, h) for p in range(2) for h in range(2)]
    first = [part(left, fa, 0, 0, 0, 0)] + first[:2] + [part(left, fa, 1, 0, 1, 1)] + first[2:] + [select]
    first += [part(fold_cols, p, rc) for p in range(2) for rc in range(0, HALF, ROWS)]
    middle = [part(right, fb, 0, 1, 0, 3), part(right, fb, 1, 1, 1, 4)]
    middle += [part(misfit, q, rc) for q in range(2) for rc in range(0, SIDE, ROWS)]
    middle += [part(right, fa, 2, 0, 0, 5), part(right, fa, 3, 0, 1, 6)]
    middle += [part(unfold_cols, p, rc) for p in range(2) for rc in range(0, HALF, ROWS)]
    middle += [part(left, fb, 3, 1, 0, 7), part(left, fb, 4, 1, 1, 8)]
    return first, middle


def grad_steps(r, c, base, grad, probe, pgrad, patch, fb):
    j = c // HALF - base
    s = c % HALF
    lane = lax.broadcasted_iota(jnp.int32, (ROWS, HALF), 1)
    below_shift = lane < s

    def chunk(rc, t):
        rows = pl.ds(t * HALF + rc, ROWS)
        pieces = []
        for h in range(2):
            cols = pl.ds(h * HALF, HALF)
            er = fb[3, pl.ds(rc, ROWS), cols]
            ei = fb[3, pl.ds(HALF + rc, ROWS), cols]
            dr = fb[4, pl.ds(rc, ROWS), cols]
            di = fb[4, pl.ds(HALF + rc, ROWS), cols]
            br, bi = (er + dr, ei + di) if t == 0 else (er - dr, ei - di)
            qr = probe[0, rows, cols]
            qi = probe[1, rows, cols]
            pr = patch[0, h, rows, :]
            pi = patch[1, h, rows, :]
            pgrad[0, h, rows, :] += pr * br + pi * bi
            pgrad[1, h, rows, :] += pr * bi - pi * br
            pieces.append((qr * br + qi * bi, qr * bi - qi * br))
        target = pl.ds(r + t * HALF + rc, ROWS)
        for part in range(2):
            first = pltpu.roll(pieces[0][part], s, 1)
            second = pltpu.roll(pieces[1][part], s, 1)
            grad[part, j, target, :] += jnp.where(below_shift, 0.0, first)
            grad[part, j + 1, target, :] += jnp.where(below_shift, first, second)
            grad[part, j + 2, target, :] += jnp.where(below_shift, second, 0.0)

    return [functools.partial(chunk, rc, t) for rc in range(0, HALF, ROWS) for t in range(2)]


def interleaved(main, side):
    done = 0
    for i, step in enumerate(main):
        step()
        upto = (i + 1) * len(side) // len(main)
        for other in side[done:upto]:
            other()
        done = upto


def slots_kernel(plan, *refs):
    live, offsets, probe_in, pgrad_in, tab_in, sel_in, measured = refs[:7]
    n_in, n_out = len(plan["in"]), len(plan["out"])
    blocks = refs[7:7 + n_in]
    outs = refs[7 + n_in:7 + n_in + n_out]
    pgrad_out = refs[7 + n_in + n_out]
    pgrad, probe, tab, sel, ext, grad, meas, patch, xh, xl, fa, fb, order, sems, msems = refs[8 + n_in + n_out:]
    slots = measured.shape[0]

    early, late = [(probe_in, probe)], [(tab_in, tab), (sel_in, sel)]
    if plan["first"]:
        pgrad[...] = jnp.zeros_like(pgrad)
    else:
        late.append((pgrad_in, pgrad))
    for (kind, panel, row, panels, source, rows), block in zip(plan["in"], blocks):
        if kind == "grad":
            late.append((block, grad.at[:, pl.ds(panel, panels), pl.ds(row, block.shape[2]), :]))
            continue
        for part in range(2):
            first = block.shape[2] // HALF - panels
            for h in range(panels):
                early.append((
                    block.at[part, pl.ds(source, rows), pl.ds((first + h) * HALF, HALF)],
                    ext.at[part, panel + h, pl.ds(row, rows), :],
                ))
    loads = [pltpu.make_async_copy(*pair, sems.at[i]) for i, pair in enumerate(early + late)]
    for load in loads:
        load.start()
    for panel, panels, row, rows in plan["zero"]:
        grad[:, pl.ds(panel, panels), pl.ds(row, rows), :] = jnp.zeros((2, panels, rows, HALF), F32)

    def collect(g, n):
        order[n] = g
        r, c = offsets[0, g], offsets[1, g]
        low_r, high_r, low_c, high_c = plan["keep"]
        used = (g < live[0]) & (r >= low_r) & (r <= high_r) & (c >= low_c) & (c <= high_c)
        return n + used.astype(jnp.int32)

    total = lax.fori_loop(0, slots, collect, jnp.int32(0))

    def fetch(n):
        slot = lax.rem(n, 2)
        return [
            pltpu.make_async_copy(measured.at[order[n], :, pl.ds(h * HALF, HALF)], meas.at[slot, h], msems.at[slot, h])
            for h in range(2)
        ]

    @pl.when(total > 0)
    def _():
        for copy in fetch(0):
            copy.start()

    for load in loads[:len(early)]:
        load.wait()

    def place(n):
        g = order[n]
        return offsets[0, g], offsets[1, g]

    @pl.when(total > 0)
    def _():
        fb[pl.ds(3, 2)] = jnp.zeros((2, SIDE, SIDE), F32)
        patch[2] = jnp.zeros((2, 2, SIDE, HALF), F32)
        r, c = place(0)
        for run in cut_steps(r, c, plan["base"], ext, probe, patch.at[0], xh, xl):
            run()
        for load in loads[len(early):]:
            load.wait()

        def step(n, carry):
            @pl.when(n + 1 < total)
            def _():
                for copy in fetch(n + 1):
                    copy.start()

            for copy in fetch(n):
                copy.wait()
            first, middle = transform_steps(meas.at[lax.rem(n, 2)], tab, sel, xh, xl, fa, fb)
            r, c = place(jnp.maximum(n - 1, 0))
            interleaved(
                first, grad_steps(r, c, plan["base"], grad, probe, pgrad, patch.at[lax.rem(n + 2, 3)], fb)
            )
            r, c = place(jnp.minimum(n + 1, total - 1))
            interleaved(middle, cut_steps(r, c, plan["base"], ext, probe, patch.at[lax.rem(n + 1, 3)], xh, xl))
            return carry

        lax.fori_loop(0, total, step, 0)
        r, c = place(total - 1)
        for run in grad_steps(r, c, plan["base"], grad, probe, pgrad, patch.at[lax.rem(total + 2, 3)], fb):
            run()

    @pl.when(total == 0)
    def _():
        for load in loads[len(early):]:
            load.wait()

    stores = [pltpu.make_async_copy(pgrad, pgrad_out, sems.at[0])]
    for (kind, panel, row, panels), out in zip(plan["out"], outs):
        if kind == "grad":
            pairs = [(grad.at[:, pl.ds(panel, panels), pl.ds(row, out.shape[2]), :], out)]
        else:
            here = pl.ds(panel, panels), pl.ds(row, out.shape[1])
            if kind == "tile":
                grad[:, *here, :] = ext[:, *here, :] - 0.25 * grad[:, *here, :]
            pairs = []
            for part in range(2):
                first = out.shape[2] // HALF - panels
                for h in range(panels):
                    pairs.append((
                        grad.at[part, panel + h, pl.ds(row, out.shape[1]), :],
                        out.at[part, :, pl.ds((first + h) * HALF, HALF)],
                    ))
        for source, target in pairs:
            stores.append(pltpu.make_async_copy(source, target, sems.at[len(stores)]))
    for store in stores:
        store.start()
    for store in stores:
        store.wait()


PLAN_OWN = {
    "base": 0, "panels": 5, "keep": (0, SIDE, 0, SIDE), "first": True,
    "in": [("ext", 0, 0, 4, 0, TILE)],
    "zero": [(0, 4, 0, TILE)],
    "out": [("tile", 0, 0, 2), ("grad", 0, SIDE, 2), ("grad", 2, 0, 2)],
    "shapes": [(2, SIDE, SIDE), (2, 2, SIDE, HALF), (2, 2, TILE, HALF)],
}
PLAN_RIGHT = {
    "base": 2, "panels": 4, "keep": (0, SIDE, SIDE + 1, TILE), "first": False,
    "in": [("ext", 0, 0, 2, 0, TILE), ("ext", 2, 0, 2, 0, TILE), ("grad", 0, 0, 2, 0, TILE)],
    "zero": [(2, 2, 0, TILE)],
    "out": [("tile", 0, 0, 2), ("array", 2, 0, 2), ("grad", 0, SIDE, 4)],
    "shapes": [(2, SIDE, SIDE), (2, SIDE, SIDE), (2, 4, SIDE, HALF)],
}
PLAN_LOWER = {
    "base": 0, "panels": 6, "keep": (SIDE + 1, TILE, 0, TILE), "first": False,
    "in": [
        ("ext", 0, SIDE, 4, SIDE, SIDE), ("ext", 0, TILE, 4, 0, SIDE), ("ext", 4, SIDE, 2, SIDE, SIDE),
        ("ext", 4, TILE, 2, 0, SIDE), ("grad", 0, SIDE, 2, 0, SIDE), ("grad", 2, SIDE, 4, 0, SIDE),
    ],
    "zero": [(0, 6, TILE, SIDE)],
    "out": [
        ("array", 4, TILE, 2), ("array", 4, SIDE, 2), ("array", 0, TILE, 2), ("array", 2, TILE, 2), ("tile", 0, SIDE, 4),
    ],
    "shapes": [(2, SIDE, SIDE), (2, SIDE, SIDE), (2, SIDE, SIDE), (2, SIDE, SIDE), (2, SIDE, TILE)],
}


def slots_call(plan, live, offsets, probe, probe_grad, measured, blocks):
    tables, select = dft_tables()
    any_spec = pl.BlockSpec(memory_space=pl.ANY)
    smem = pl.BlockSpec(memory_space=pltpu.SMEM)
    shapes = plan["shapes"] + [(2, 2, SIDE, HALF)]
    rows, panels = WIDE, plan["panels"]
    return pl.pallas_call(
        functools.partial(slots_kernel, plan),
        out_shape=[jax.ShapeDtypeStruct(s, F32) for s in shapes],
        in_specs=[smem, smem] + [any_spec] * (5 + len(blocks)),
        out_specs=[any_spec] * len(shapes),
        scratch_shapes=[
            pltpu.VMEM((2, 2, SIDE, HALF), F32),
            pltpu.VMEM(probe.shape, F32),
            pltpu.VMEM(tables.shape, BF16),
            pltpu.VMEM(select.shape, BF16),
            pltpu.VMEM((2, panels, rows, HALF), F32),
            pltpu.VMEM((2, panels, rows, HALF), F32),
            pltpu.VMEM((2, 2, SIDE, HALF), F32),
            pltpu.VMEM((3, 2, 2, SIDE, HALF), F32),
            pltpu.VMEM((9, SIDE, SIDE), BF16),
            pltpu.VMEM((9, SIDE, SIDE), BF16),
            pltpu.VMEM((4, SIDE, SIDE), F32),
            pltpu.VMEM((5, SIDE, SIDE), F32),
            pltpu.SMEM((measured.shape[0],), jnp.int32),
            pltpu.SemaphoreType.DMA((32,)),
            pltpu.SemaphoreType.DMA((2, 2)),
        ],
        compiler_params=pltpu.CompilerParams(vmem_limit_bytes=56 * 1024 * 1024),
        cost_estimate=pl.CostEstimate(flops=2**20, bytes_accessed=2**20, transcendentals=0),
    )(live, offsets.T, probe, probe_grad, jnp.asarray(tables), jnp.asarray(select), measured, *blocks)


ROW_AXES = ("z", "y_lo", "core")
COL_AXES = ("x", "y_hi")
NEAR_AXES = ("z", "core", "x")
FAR_AXES = ("y_lo", "y_hi")


def passed_along(block, axes, distance):
    devices = range(lax.axis_size(axes))
    route = [(i - distance, i) for i in devices if i - distance in devices]
    return lax.ppermute(block, axes, route)


def passed_across(block, distance):
    rows, cols = lax.axis_size(ROW_AXES), lax.axis_size(COL_AXES)
    pairs = []
    for i in range(rows):
        for j in range(cols):
            if 0 <= i - distance < rows and 0 <= j - distance < cols:
                pairs.append(((i - distance) * cols + j - distance, i * cols + j))
    return lax.ppermute(block, ROW_AXES + COL_AXES, pairs)


def update_kernel(
    scale, top_left, top_right, lower, left_top, left_low, above_left, above_right, across, probe, total, out, probe_out,
    tile_v, left_v, above_v, across_v, probe_v, total_v, sems, out_sems,
):
    top, low = pl.ds(0, SIDE), pl.ds(SIDE, TILE - SIDE)
    first, second = pl.ds(0, SIDE), pl.ds(SIDE, TILE - SIDE)
    pairs = [
        (top_left, tile_v.at[:, top, first]), (top_right, tile_v.at[:, top, second]), (lower, tile_v.at[:, low, :]),
        (above_left, above_v.at[0]), (above_right, above_v.at[1]), (across, across_v), (left_top, left_v.at[0]),
        (left_low, left_v.at[1]), (probe, probe_v), (total, total_v),
    ]
    loads = [pltpu.make_async_copy(*pair, sems.at[i]) for i, pair in enumerate(pairs)]
    for load in loads:
        load.start()
    for load in loads:
        load.wait()
    stores = []
    for part in range(2):
        tile_v[part, top, first] -= 0.25 * (left_v[0, part] + (above_v[0, part] + across_v[part]))
        tile_v[part, top, second] -= 0.25 * above_v[1, part]
        tile_v[part, low, first] -= 0.25 * left_v[1, part]
        stores.append(pltpu.make_async_copy(tile_v.at[part], out.at[part], out_sems.at[part]))
        stores[-1].start()
    for part in range(2):
        for h in range(2):
            cols = pl.ds(h * HALF, HALF)
            probe_v[part, :, cols] -= scale * total_v[part, h]
    stores.append(pltpu.make_async_copy(probe_v, probe_out, out_sems.at[2]))
    stores[-1].start()
    for store in stores:
        store.wait()


def update(scale, *parts):
    any_spec = pl.BlockSpec(memory_space=pl.ANY)
    probe = parts[-2]
    return pl.pallas_call(
        functools.partial(update_kernel, scale),
        out_shape=[jax.ShapeDtypeStruct((2, TILE, TILE), F32), jax.ShapeDtypeStruct(probe.shape, F32)],
        in_specs=[any_spec] * len(parts),
        out_specs=[any_spec] * 2,
        scratch_shapes=[
            pltpu.VMEM((2, TILE, TILE), F32),
            pltpu.VMEM((2, 2, SIDE, SIDE), F32),
            pltpu.VMEM((2, 2, SIDE, SIDE), F32),
            pltpu.VMEM((2, SIDE, SIDE), F32),
            pltpu.VMEM(probe.shape, F32),
            pltpu.VMEM(parts[-1].shape, F32),
            pltpu.SemaphoreType.DMA((10,)),
            pltpu.SemaphoreType.DMA((3,)),
        ],
        compiler_params=pltpu.CompilerParams(vmem_limit_bytes=56 * 1024 * 1024),
        cost_estimate=pl.CostEstimate(flops=2**20, bytes_accessed=2**20, transcendentals=0),
    )(*parts)


def total_over_all(x, before):
    near = lax.axis_size(NEAR_AXES)
    blocks = x.reshape(-1, 8, HALF)
    shares = lax.all_to_all(blocks, NEAR_AXES, 0, 0, tiled=True)
    share = jnp.sum(shares.reshape(near, -1, 8, HALF), axis=0)
    far = lax.axis_size(FAR_AXES)
    copies = jnp.broadcast_to(share[None], (far,) + share.shape).reshape((-1,) + share.shape[1:])
    share = lax.all_to_all(copies, FAR_AXES, 0, 0, tiled=True)
    share = jnp.sum(share.reshape((far, -1) + share.shape[1:]), axis=0)
    share, before = lax.optimization_barrier((share, before))
    copies = jnp.broadcast_to(share[None], (near,) + share.shape).reshape(blocks.shape)
    return lax.all_to_all(copies, NEAR_AXES, 0, 0, tiled=True).reshape(x.shape), before


def body(object_field, probe, measured, offsets, live):
    side = probe.shape[1]
    half = side // 2
    positions = measured.shape[0] * lax.axis_size(ROW_AXES) * lax.axis_size(COL_AXES)
    right = passed_along(object_field[:, :, :side], COL_AXES, -1)

    def call(plan, probe_grad, blocks):
        return slots_call(plan, live, offsets, probe, probe_grad, measured, blocks)

    top_left, grad_left, grad_right, probe_grad = call(PLAN_OWN, jnp.zeros((2, 2, 8, half), F32), [object_field])
    below_source, corner_source, grad_right = lax.optimization_barrier(
        (object_field[:, :side, :], object_field[:, :side, :side], grad_right)
    )
    below = passed_along(below_source, ROW_AXES, -1)
    corner = passed_across(corner_source, -1)
    top_right, right_top, grad_low, probe_grad = call(PLAN_RIGHT, probe_grad, [object_field, right, grad_right])
    below, corner, grad_low, right_top = lax.optimization_barrier((below, corner, grad_low, right_top))
    left_top = passed_along(right_top, COL_AXES, 1)
    to_across, right_low, below_left, below_right, lower, probe_grad = call(
        PLAN_LOWER, probe_grad, [object_field, below, right, corner, grad_left, grad_low]
    )
    from_across = passed_across(to_across, 1)
    above_left = passed_along(below_left, ROW_AXES, 1)
    above_right = passed_along(below_right, ROW_AXES, 1)
    left_top, probe_grad = lax.optimization_barrier((left_top, probe_grad))
    total_grad, (from_across, right_low) = total_over_all(probe_grad, (from_across, right_low))
    left_low = passed_along(right_low, COL_AXES, 1)
    object_next, probe_next = update(
        1.0 / math.sqrt(positions), top_left, top_right, lower, left_top, left_low, above_left, above_right, from_across,
        probe, total_grad,
    )
    return (object_next, probe_next)


def solution(mesh):
    whole = jax.sharding.Mesh(mesh.devices.reshape(4, 2, 2, 4, 2), ROW_AXES + COL_AXES)
    both = ROW_AXES + COL_AXES
    placed = (P(None, ROW_AXES, COL_AXES), P(), P(both, None), P(both), P(both))
    return jax.shard_map(
        body, mesh=whole, in_specs=placed, out_specs=(P(None, ROW_AXES, COL_AXES), P()), check_vma=False
    )
```

```python
import functools
import math

import jax
import jax.numpy as jnp
import ml_dtypes
import numpy as np
from jax import lax
from jax.experimental import pallas as pl
from jax.experimental.pallas import tpu as pltpu
from jax.sharding import PartitionSpec as P

BF16 = jnp.bfloat16
F32 = jnp.float32
SIDE = 256
HALF = 128
TILE = 512
WIDE = TILE + SIDE
ROWS = 64


def split_np(table):
    high = table.astype(ml_dtypes.bfloat16)
    low = (table - high.astype(np.float64)).astype(ml_dtypes.bfloat16)
    return high, low


def dft_tables():
    k = np.arange(HALF)[:, None]
    n = np.arange(HALF)[None, :]
    forward = []
    backward = []
    for parity in range(2):
        angle = -2.0 * math.pi * ((n * (2 * k + parity)) % SIDE) / SIDE
        cos = np.cos(angle) / math.sqrt(SIDE)
        sin = np.sin(angle) / math.sqrt(SIDE)
        stacked = np.block([[cos, -sin], [sin, cos]])
        forward.extend(split_np(stacked))
        backward.extend(split_np(stacked.T))
    tables = np.stack(forward + backward).reshape(2, 2, 2, SIDE, SIDE)
    order = np.concatenate([np.arange(0, SIDE, 2), np.arange(1, SIDE, 2)])
    select = np.zeros((SIDE, SIDE), np.float32)
    select[order, np.arange(SIDE)] = 1.0
    return tables, select.astype(ml_dtypes.bfloat16)


def split(x):
    high = x.astype(BF16)
    low = (x - high.astype(F32)).astype(BF16)
    return high, low


def mm(a, b):
    return lax.dot_general(a, b, (((1,), (0,)), ((), ())), preferred_element_type=F32)


def left3(high, low, x_high, x_low):
    return mm(high, x_high) + (mm(high, x_low) + mm(low, x_high))


def right3(x_high, x_low, high, low):
    return mm(x_high, high) + (mm(x_low, high) + mm(x_high, low))


def cut_steps(r, c, base, ext, probe, patch, xh, xl):
    j = c // HALF - base
    back_shift = lax.rem(HALF - c % HALF, HALF)
    lane = lax.broadcasted_iota(jnp.int32, (ROWS, HALF), 1)
    take_first = lane < HALF - c % HALF

    def chunk(rc):
        wave = []
        for t in range(2):
            cut = []
            rows = pl.ds(t * HALF + rc, ROWS)
            for part in range(2):
                rolled = [
                    pltpu.roll(ext[part, j + h, pl.ds(r + t * HALF + rc, ROWS), :], back_shift, 1) for h in range(3)
                ]
                halves = [jnp.where(take_first, rolled[h], rolled[h + 1]) for h in range(2)]
                for h in range(2):
                    patch[part, h, rows, :] = halves[h]
                cut.append(halves)
            here = []
            for h in range(2):
                cols = pl.ds(h * HALF, HALF)
                qr = probe[0, rows, cols]
                qi = probe[1, rows, cols]
                here.append((qr * cut[0][h] - qi * cut[1][h], qr * cut[1][h] + qi * cut[0][h]))
            wave.append(here)
        for h in range(2):
            for part in range(2):
                top = wave[0][h][part]
                bottom = wave[1][h][part]
                for p, folded in enumerate((top + bottom, top - bottom)):
                    high, low = split(folded)
                    xh[p, pl.ds(part * HALF + rc, ROWS), pl.ds(h * HALF, HALF)] = high
                    xl[p, pl.ds(part * HALF + rc, ROWS), pl.ds(h * HALF, HALF)] = low

    return [functools.partial(chunk, rc) for rc in range(0, HALF, ROWS)]


def transform_steps(meas, tab, sel, xh, xl, fa, fb):
    first, middle = [], []

    def left(out, k, table, p, source):
        out[k] = left3(tab[table, p, 0], tab[table, p, 1], xh[source], xl[source])

    def right(out, k, table, q, source):
        out[k] = right3(xh[source], xl[source], tab[table, q, 0], tab[table, q, 1])

    def sort_measured(p, h):
        high, low = split(meas[h, pl.ds(p, HALF, stride=2), :])
        xh[2, pl.ds(p * HALF, HALF), pl.ds(h * HALF, HALF)] = high
        xl[2, pl.ds(p * HALF, HALF), pl.ds(h * HALF, HALF)] = low

    def select():
        fb[2] = mm(xh[2], sel[...]) + mm(xl[2], sel[...])

    def fold_cols(p, rc):
        for part in range(2):
            rows = pl.ds(part * HALF + rc, ROWS)
            near = fa[p, rows, pl.ds(0, HALF)]
            far = fa[p, rows, pl.ds(HALF, HALF)]
            for q, folded in enumerate((near + far, near - far)):
                high, low = split(folded)
                xh[3 + q, pl.ds(p * HALF + rc, ROWS), pl.ds(part * HALF, HALF)] = high
                xl[3 + q, pl.ds(p * HALF + rc, ROWS), pl.ds(part * HALF, HALF)] = low

    def misfit(q, rc):
        rows = pl.ds(rc, ROWS)
        re = fb[q, rows, pl.ds(0, HALF)]
        im = fb[q, rows, pl.ds(HALF, HALF)]
        miss = re * re + im * im - fb[2, rows, pl.ds(q * HALF, HALF)]
        for part, value in enumerate((miss * re, miss * im)):
            high, low = split(value)
            xh[5 + q, rows, pl.ds(part * HALF, HALF)] = high
            xl[5 + q, rows, pl.ds(part * HALF, HALF)] = low

    def unfold_cols(p, rc):
        rows = pl.ds(p * HALF + rc, ROWS)
        for part in range(2):
            cols = pl.ds(part * HALF, HALF)
            even = fa[2, rows, cols]
            odd = fa[3, rows, cols]
            for h, value in enumerate((even + odd, even - odd)):
                high, low = split(value)
                xh[7 + p, pl.ds(part * HALF + rc, ROWS), pl.ds(h * HALF, HALF)] = high
                xl[7 + p, pl.ds(part * HALF + rc, ROWS), pl.ds(h * HALF, HALF)] = low

    part = functools.partial
    first = [part(sort_measured, p, h) for p in range(2) for h in range(2)]
    first = [part(left, fa, 0, 0, 0, 0)] + first[:2] + [part(left, fa, 1, 0, 1, 1)] + first[2:] + [select]
    first += [part(fold_cols, p, rc) for p in range(2) for rc in range(0, HALF, ROWS)]
    middle = [part(right, fb, 0, 1, 0, 3), part(right, fb, 1, 1, 1, 4)]
    middle += [part(misfit, q, rc) for q in range(2) for rc in range(0, SIDE, ROWS)]
    middle += [part(right, fa, 2, 0, 0, 5), part(right, fa, 3, 0, 1, 6)]
    middle += [part(unfold_cols, p, rc) for p in range(2) for rc in range(0, HALF, ROWS)]
    middle += [part(left, fb, 3, 1, 0, 7), part(left, fb, 4, 1, 1, 8)]
    return first, middle


def grad_steps(r, c, base, grad, probe, pgrad, patch, fb):
    j = c // HALF - base
    s = c % HALF
    lane = lax.broadcasted_iota(jnp.int32, (ROWS, HALF), 1)
    below_shift = lane < s

    def chunk(rc, t):
        rows = pl.ds(t * HALF + rc, ROWS)
        pieces = []
        for h in range(2):
            cols = pl.ds(h * HALF, HALF)
            er = fb[3, pl.ds(rc, ROWS), cols]
            ei = fb[3, pl.ds(HALF + rc, ROWS), cols]
            dr = fb[4, pl.ds(rc, ROWS), cols]
            di = fb[4, pl.ds(HALF + rc, ROWS), cols]
            br, bi = (er + dr, ei + di) if t == 0 else (er - dr, ei - di)
            qr = probe[0, rows, cols]
            qi = probe[1, rows, cols]
            pr = patch[0, h, rows, :]
            pi = patch[1, h, rows, :]
            pgrad[0, h, rows, :] += pr * br + pi * bi
            pgrad[1, h, rows, :] += pr * bi - pi * br
            pieces.append((qr * br + qi * bi, qr * bi - qi * br))
        target = pl.ds(r + t * HALF + rc, ROWS)
        for part in range(2):
            first = pltpu.roll(pieces[0][part], s, 1)
            second = pltpu.roll(pieces[1][part], s, 1)
            grad[part, j, target, :] += jnp.where(below_shift, 0.0, first)
            grad[part, j + 1, target, :] += jnp.where(below_shift, first, second)
            grad[part, j + 2, target, :] += jnp.where(below_shift, second, 0.0)

    return [functools.partial(chunk, rc, t) for rc in range(0, HALF, ROWS) for t in range(2)]


def interleaved(main, side):
    done = 0
    for i, step in enumerate(main):
        step()
        upto = (i + 1) * len(side) // len(main)
        for other in side[done:upto]:
            other()
        done = upto


def slots_kernel(plan, *refs):
    live, offsets, probe_in, pgrad_in, tab_in, sel_in, measured = refs[:7]
    n_in, n_out = len(plan["in"]), len(plan["out"])
    blocks = refs[7:7 + n_in]
    outs = refs[7 + n_in:7 + n_in + n_out]
    pgrad_out = refs[7 + n_in + n_out]
    pgrad, probe, tab, sel, ext, grad, meas, patch, xh, xl, fa, fb, order, sems, msems, copy_sems = refs[8 + n_in + n_out:]
    slots = measured.shape[0]

    early, late = [(probe_in, probe)], [(tab_in, tab), (sel_in, sel)]
    if plan["first"]:
        pgrad[...] = jnp.zeros_like(pgrad)
    else:
        late.append((pgrad_in, pgrad))
    for (kind, panel, row, panels, source, rows), block in zip(plan["in"], blocks):
        if kind == "grad":
            late.append((block, grad.at[:, pl.ds(panel, panels), pl.ds(row, block.shape[2]), :]))
            continue
        for part in range(2):
            first = block.shape[2] // HALF - panels
            for h in range(panels):
                early.append((
                    block.at[part, pl.ds(source, rows), pl.ds((first + h) * HALF, HALF)],
                    ext.at[part, panel + h, pl.ds(row, rows), :],
                ))
    loads = [pltpu.make_async_copy(*pair, sems.at[i]) for i, pair in enumerate(early + late)]
    for load in loads:
        load.start()
    for panel, panels, row, rows in plan["zero"]:
        grad[:, pl.ds(panel, panels), pl.ds(row, rows), :] = jnp.zeros((2, panels, rows, HALF), F32)

    def collect(g, n):
        order[n] = g
        r, c = offsets[0, g], offsets[1, g]
        low_r, high_r, low_c, high_c = plan["keep"]
        used = (g < live[0]) & (r >= low_r) & (r <= high_r) & (c >= low_c) & (c <= high_c)
        return n + used.astype(jnp.int32)

    total = lax.fori_loop(0, slots, collect, jnp.int32(0))

    def fetch(n):
        slot = lax.rem(n, 2)
        return [
            pltpu.make_async_copy(measured.at[order[n], :, pl.ds(h * HALF, HALF)], meas.at[slot, h], msems.at[slot, h])
            for h in range(2)
        ]

    @pl.when(total > 0)
    def _():
        for copy in fetch(0):
            copy.start()

    for load in loads[:len(early)]:
        load.wait()
    copies = []
    for (kind, panel, row, panels), out in zip(plan["out"], outs):
        if kind == "copy":
            for part in range(2):
                for h in range(panels):
                    copies.append(pltpu.make_async_copy(
                        ext.at[part, panel + h, pl.ds(row, out.shape[1]), :], out.at[part, :, pl.ds(h * HALF, HALF)],
                        copy_sems.at[len(copies)],
                    ))
    for copy in copies:
        copy.start()

    def place(n):
        g = order[n]
        return offsets[0, g], offsets[1, g]

    @pl.when(total > 0)
    def _():
        fb[pl.ds(3, 2)] = jnp.zeros((2, SIDE, SIDE), F32)
        patch[2] = jnp.zeros((2, 2, SIDE, HALF), F32)
        r, c = place(0)
        for run in cut_steps(r, c, plan["base"], ext, probe, patch.at[0], xh, xl):
            run()
        for load in loads[len(early):]:
            load.wait()

        def step(n, carry):
            @pl.when(n + 1 < total)
            def _():
                for copy in fetch(n + 1):
                    copy.start()

            for copy in fetch(n):
                copy.wait()
            first, middle = transform_steps(meas.at[lax.rem(n, 2)], tab, sel, xh, xl, fa, fb)
            r, c = place(jnp.maximum(n - 1, 0))
            interleaved(
                first, grad_steps(r, c, plan["base"], grad, probe, pgrad, patch.at[lax.rem(n + 2, 3)], fb)
            )
            r, c = place(jnp.minimum(n + 1, total - 1))
            interleaved(middle, cut_steps(r, c, plan["base"], ext, probe, patch.at[lax.rem(n + 1, 3)], xh, xl))
            return carry

        lax.fori_loop(0, total, step, 0)
        r, c = place(total - 1)
        for run in grad_steps(r, c, plan["base"], grad, probe, pgrad, patch.at[lax.rem(total + 2, 3)], fb):
            run()

    @pl.when(total == 0)
    def _():
        for load in loads[len(early):]:
            load.wait()

    stores = [pltpu.make_async_copy(pgrad, pgrad_out, sems.at[0])]
    for (kind, panel, row, panels), out in zip(plan["out"], outs):
        if kind == "copy":
            continue
        if kind == "grad":
            pairs = [(grad.at[:, pl.ds(panel, panels), pl.ds(row, out.shape[2]), :], out)]
        else:
            here = pl.ds(panel, panels), pl.ds(row, out.shape[1])
            if kind == "tile":
                grad[:, *here, :] = ext[:, *here, :] - 0.25 * grad[:, *here, :]
            pairs = []
            for part in range(2):
                first = out.shape[2] // HALF - panels
                for h in range(panels):
                    pairs.append((
                        grad.at[part, panel + h, pl.ds(row, out.shape[1]), :],
                        out.at[part, :, pl.ds((first + h) * HALF, HALF)],
                    ))
        for source, target in pairs:
            stores.append(pltpu.make_async_copy(source, target, sems.at[len(stores)]))
    for store in stores:
        store.start()
    for store in stores + copies:
        store.wait()


PLAN_OWN = {
    "base": 0, "panels": 5, "keep": (0, SIDE, 0, SIDE), "first": True,
    "in": [("ext", 0, 0, 4, 0, TILE)],
    "zero": [(0, 4, 0, TILE)],
    "out": [("tile", 0, 0, 2), ("grad", 0, SIDE, 2), ("grad", 2, 0, 2), ("copy", 0, 0, 4), ("copy", 0, 0, 2)],
    "shapes": [(2, SIDE, SIDE), (2, 2, SIDE, HALF), (2, 2, TILE, HALF), (2, SIDE, TILE), (2, SIDE, SIDE)],
}
PLAN_RIGHT = {
    "base": 2, "panels": 4, "keep": (0, SIDE, SIDE + 1, TILE), "first": False,
    "in": [("ext", 0, 0, 2, 0, TILE), ("ext", 2, 0, 2, 0, TILE), ("grad", 0, 0, 2, 0, TILE)],
    "zero": [(2, 2, 0, TILE)],
    "out": [("tile", 0, 0, 2), ("array", 2, 0, 2), ("grad", 0, SIDE, 4)],
    "shapes": [(2, SIDE, SIDE), (2, SIDE, SIDE), (2, 4, SIDE, HALF)],
}
PLAN_LOWER = {
    "base": 0, "panels": 6, "keep": (SIDE + 1, TILE, 0, TILE), "first": False,
    "in": [
        ("ext", 0, SIDE, 4, SIDE, SIDE), ("ext", 0, TILE, 4, 0, SIDE), ("ext", 4, SIDE, 2, SIDE, SIDE),
        ("ext", 4, TILE, 2, 0, SIDE), ("grad", 0, SIDE, 2, 0, SIDE), ("grad", 2, SIDE, 4, 0, SIDE),
    ],
    "zero": [(0, 6, TILE, SIDE)],
    "out": [
        ("array", 4, TILE, 2), ("array", 4, SIDE, 2), ("array", 0, TILE, 2), ("array", 2, TILE, 2), ("tile", 0, SIDE, 4),
    ],
    "shapes": [(2, SIDE, SIDE), (2, SIDE, SIDE), (2, SIDE, SIDE), (2, SIDE, SIDE), (2, SIDE, TILE)],
}


def slots_call(plan, live, offsets, probe, probe_grad, measured, blocks):
    tables, select = dft_tables()
    any_spec = pl.BlockSpec(memory_space=pl.ANY)
    smem = pl.BlockSpec(memory_space=pltpu.SMEM)
    shapes = plan["shapes"] + [(2, 2, SIDE, HALF)]
    rows, panels = WIDE, plan["panels"]
    return pl.pallas_call(
        functools.partial(slots_kernel, plan),
        out_shape=[jax.ShapeDtypeStruct(s, F32) for s in shapes],
        in_specs=[smem, smem] + [any_spec] * (5 + len(blocks)),
        out_specs=[any_spec] * len(shapes),
        scratch_shapes=[
            pltpu.VMEM((2, 2, SIDE, HALF), F32),
            pltpu.VMEM(probe.shape, F32),
            pltpu.VMEM(tables.shape, BF16),
            pltpu.VMEM(select.shape, BF16),
            pltpu.VMEM((2, panels, rows, HALF), F32),
            pltpu.VMEM((2, panels, rows, HALF), F32),
            pltpu.VMEM((2, 2, SIDE, HALF), F32),
            pltpu.VMEM((3, 2, 2, SIDE, HALF), F32),
            pltpu.VMEM((9, SIDE, SIDE), BF16),
            pltpu.VMEM((9, SIDE, SIDE), BF16),
            pltpu.VMEM((4, SIDE, SIDE), F32),
            pltpu.VMEM((5, SIDE, SIDE), F32),
            pltpu.SMEM((measured.shape[0],), jnp.int32),
            pltpu.SemaphoreType.DMA((32,)),
            pltpu.SemaphoreType.DMA((2, 2)),
            pltpu.SemaphoreType.DMA((12,)),
        ],
        compiler_params=pltpu.CompilerParams(vmem_limit_bytes=56 * 1024 * 1024),
        cost_estimate=pl.CostEstimate(flops=2**20, bytes_accessed=2**20, transcendentals=0),
    )(live, offsets.T, probe, probe_grad, jnp.asarray(tables), jnp.asarray(select), measured, *blocks)


ROW_AXES = ("z", "y_lo", "core")
COL_AXES = ("x", "y_hi")
NEAR_AXES = ("z", "core", "x")
FAR_AXES = ("y_lo", "y_hi")


def passed_along(block, axes, distance):
    devices = range(lax.axis_size(axes))
    route = [(i - distance, i) for i in devices if i - distance in devices]
    return lax.ppermute(block, axes, route)


def passed_across(block, distance):
    rows, cols = lax.axis_size(ROW_AXES), lax.axis_size(COL_AXES)
    pairs = []
    for i in range(rows):
        for j in range(cols):
            if 0 <= i - distance < rows and 0 <= j - distance < cols:
                pairs.append(((i - distance) * cols + j - distance, i * cols + j))
    return lax.ppermute(block, ROW_AXES + COL_AXES, pairs)


def update_kernel(
    scale, top_left, top_right, lower, left_top, left_low, above_left, above_right, across, probe, total, out, probe_out,
    tile_v, left_v, above_v, across_v, probe_v, total_v, sems, out_sems,
):
    top, low = pl.ds(0, SIDE), pl.ds(SIDE, TILE - SIDE)
    first, second = pl.ds(0, SIDE), pl.ds(SIDE, TILE - SIDE)
    pairs = [
        (top_left, tile_v.at[:, top, first]), (top_right, tile_v.at[:, top, second]), (lower, tile_v.at[:, low, :]),
        (above_left, above_v.at[0]), (above_right, above_v.at[1]), (across, across_v), (left_top, left_v.at[0]),
        (left_low, left_v.at[1]), (probe, probe_v), (total, total_v),
    ]
    loads = [pltpu.make_async_copy(*pair, sems.at[i]) for i, pair in enumerate(pairs)]
    for load in loads:
        load.start()
    for load in loads:
        load.wait()
    stores = []
    for part in range(2):
        tile_v[part, top, first] -= 0.25 * (left_v[0, part] + (above_v[0, part] + across_v[part]))
        tile_v[part, top, second] -= 0.25 * above_v[1, part]
        tile_v[part, low, first] -= 0.25 * left_v[1, part]
        stores.append(pltpu.make_async_copy(tile_v.at[part], out.at[part], out_sems.at[part]))
        stores[-1].start()
    for part in range(2):
        for h in range(2):
            cols = pl.ds(h * HALF, HALF)
            probe_v[part, :, cols] -= scale * total_v[part, h]
    stores.append(pltpu.make_async_copy(probe_v, probe_out, out_sems.at[2]))
    stores[-1].start()
    for store in stores:
        store.wait()


def update(scale, *parts):
    any_spec = pl.BlockSpec(memory_space=pl.ANY)
    probe = parts[-2]
    return pl.pallas_call(
        functools.partial(update_kernel, scale),
        out_shape=[jax.ShapeDtypeStruct((2, TILE, TILE), F32), jax.ShapeDtypeStruct(probe.shape, F32)],
        in_specs=[any_spec] * len(parts),
        out_specs=[any_spec] * 2,
        scratch_shapes=[
            pltpu.VMEM((2, TILE, TILE), F32),
            pltpu.VMEM((2, 2, SIDE, SIDE), F32),
            pltpu.VMEM((2, 2, SIDE, SIDE), F32),
            pltpu.VMEM((2, SIDE, SIDE), F32),
            pltpu.VMEM(probe.shape, F32),
            pltpu.VMEM(parts[-1].shape, F32),
            pltpu.SemaphoreType.DMA((10,)),
            pltpu.SemaphoreType.DMA((3,)),
        ],
        compiler_params=pltpu.CompilerParams(vmem_limit_bytes=56 * 1024 * 1024),
        cost_estimate=pl.CostEstimate(flops=2**20, bytes_accessed=2**20, transcendentals=0),
    )(*parts)


def total_over_all(x, before):
    near = lax.axis_size(NEAR_AXES)
    blocks = x.reshape(-1, 8, HALF)
    shares = lax.all_to_all(blocks, NEAR_AXES, 0, 0, tiled=True)
    share = jnp.sum(shares.reshape(near, -1, 8, HALF), axis=0)
    far = lax.axis_size(FAR_AXES)
    copies = jnp.broadcast_to(share[None], (far,) + share.shape).reshape((-1,) + share.shape[1:])
    share = lax.all_to_all(copies, FAR_AXES, 0, 0, tiled=True)
    share = jnp.sum(share.reshape((far, -1) + share.shape[1:]), axis=0)
    share, before = lax.optimization_barrier((share, before))
    copies = jnp.broadcast_to(share[None], (near,) + share.shape).reshape(blocks.shape)
    return lax.all_to_all(copies, NEAR_AXES, 0, 0, tiled=True).reshape(x.shape), before


def body(object_field, probe, measured, offsets, live):
    side = probe.shape[1]
    half = side // 2
    positions = measured.shape[0] * lax.axis_size(ROW_AXES) * lax.axis_size(COL_AXES)
    right = passed_along(object_field[:, :, :side], COL_AXES, -1)

    def call(plan, probe_grad, blocks):
        return slots_call(plan, live, offsets, probe, probe_grad, measured, blocks)

    top_left, grad_left, grad_right, to_above, to_corner, probe_grad = call(PLAN_OWN, probe, [object_field])
    below = passed_along(to_above, ROW_AXES, -1)
    corner = passed_across(to_corner, -1)
    top_right, right_top, grad_low, probe_grad = call(PLAN_RIGHT, probe_grad, [object_field, right, grad_right])
    below, corner, grad_low, right_top = lax.optimization_barrier((below, corner, grad_low, right_top))
    left_top = passed_along(right_top, COL_AXES, 1)
    to_across, right_low, below_left, below_right, lower, probe_grad = call(
        PLAN_LOWER, probe_grad, [object_field, below, right, corner, grad_left, grad_low]
    )
    from_across = passed_across(to_across, 1)
    above_left = passed_along(below_left, ROW_AXES, 1)
    above_right = passed_along(below_right, ROW_AXES, 1)
    left_top, probe_grad = lax.optimization_barrier((left_top, probe_grad))
    total_grad, (from_across, right_low) = total_over_all(probe_grad, (from_across, right_low))
    left_low = passed_along(right_low, COL_AXES, 1)
    object_next, probe_next = update(
        1.0 / math.sqrt(positions), top_left, top_right, lower, left_top, left_low, above_left, above_right, from_across,
        probe, total_grad,
    )
    return (object_next, probe_next)


def solution(mesh):
    whole = jax.sharding.Mesh(mesh.devices.reshape(4, 2, 2, 4, 2), ROW_AXES + COL_AXES)
    both = ROW_AXES + COL_AXES
    placed = (P(None, ROW_AXES, COL_AXES), P(), P(both, None), P(both), P(both))
    return jax.shard_map(
        body, mesh=whole, in_specs=placed, out_specs=(P(None, ROW_AXES, COL_AXES), P()), check_vma=False
    )
```
